768 devices in a mesh: samp: 192 (over y, z, core), var: 4 (over x).
Axes of the slice: x: 4, y: 8, z: 12, core: 2. Of those that a mesh axis runs over, the one named last changes fastest.
Arguments:
- samples: bfloat16 [98304, 8, 256], P('samp', 'var'), may hold values from -16 to 16
- estimate: float32 [8, 768, 256], P('var'), may hold values from -6 to 6
- block_rows: int32 [8, 3], replicated, may hold values from 0 to 7, as said below
- counts: int32 [8], replicated, may hold values from 1 to 3, as said below
- holder: int32 [8], replicated, may hold values from 0 to 7, each once
Outputs:
- refined: float32 [8, 768, 256], P('var', 'samp')
The draws below stay inside these ranges and needn't reach their ends.
Inputs may be any that keep to these rules, and one draw needn't show every extreme that they name: `block_rows`: row j lists block column j's pattern: slot 0 holds j, the first counts[j] slots hold distinct block rows, the remaining slots hold j; the pattern is symmetric: i is live in column j exactly when j is live in column i. `counts`: some block column has 3 live slots and some has one. `holder`: each block column is stored at exactly one position.
All inputs are finite; a program needn't handle non-finite values.
Results may differ from the reference program's by a relative error of at most 0.0004.
The reference program's roundings to bfloat16 on the way (of `weights` and `projected`) count: a program that leaves them out, or rounds other values in their place, can miss the bound.
Values may be sent and summed in bfloat16 or wider, within the bound.
A program may use at most 32 MiB of HBM per device.

```python
import math
import jax
import jax.numpy as jnp
from jax import lax

BLK = 256
KMAX = 3
ITERS = 2
NB = 8
SAMPLES = 98304


def pattern_tables(key):
    offset = jax.random.randint(jax.random.fold_in(key, 11), (), 1, NB // 2)
    include = (jax.random.randint(jax.random.fold_in(key, 12), (NB,), 0, 5) < 3).astype(jnp.int32)
    full_col = jax.random.randint(jax.random.fold_in(key, 13), (), 0, NB)
    lone_col = (full_col + NB // 2) % NB
    block_ids = jnp.arange(NB, dtype=jnp.int32)
    forced_on = (block_ids == full_col) | (block_ids == (full_col - offset) % NB)
    forced_off = (block_ids == lone_col) | (block_ids == (lone_col - offset) % NB)
    include = jnp.where(forced_on, 1, jnp.where(forced_off, 0, include))
    upper = (block_ids + offset) % NB
    lower = (block_ids - offset) % NB
    candidates = jnp.stack([block_ids, upper, lower], axis=1)
    alive = jnp.stack([jnp.ones_like(include), include, jnp.take(include, lower)], axis=1)
    order_key = (1 - alive) * 3 + jnp.arange(3, dtype=jnp.int32)[None, :]
    order = jnp.argsort(order_key, axis=1)
    listed = jnp.take_along_axis(candidates, order, axis=1)
    alive_sorted = jnp.take_along_axis(alive, order, axis=1)
    listed = jnp.where(alive_sorted == 1, listed, block_ids[:, None])
    return (listed.astype(jnp.int32), jnp.sum(alive, axis=1).astype(jnp.int32))


def draw_block_rows(key, part):
    listed, sizes = pattern_tables(key)
    return listed


def draw_counts(key, part):
    listed, sizes = pattern_tables(key)
    return sizes


def draw_samples(key, part):
    key = jax.random.fold_in(key, 5)
    key_scale, key_noise = jax.random.split(key, 2)
    columns_total = NB * BLK
    scales = jnp.exp(jax.random.uniform(key_scale, (columns_total,), jnp.float32, math.log(0.5), math.log(2.0)))
    noise = jnp.clip(jax.random.normal(key_noise, (SAMPLES, columns_total + 1), jnp.float32), -6.0, 6.0)
    mixed = noise[:, :columns_total] + 0.5 * noise[:, 1:]
    return jnp.clip(mixed * scales[None, :], -16.0, 16.0).reshape(SAMPLES, NB, BLK).astype(jnp.bfloat16)


def levels(rng, shape, pieces, low, largest):
    loudness, own = 1.0, jax.random.fold_in(rng, 6)
    for dim, blocks in pieces:
        steps = jnp.exp(jax.random.uniform(jax.random.fold_in(own, dim), (blocks,), jnp.float32, low / len(pieces), largest / len(pieces)))
        loudness = loudness * jnp.repeat(steps, shape[dim] // blocks).reshape([-1 if axis == dim else 1 for axis in range(len(shape))])
    return loudness


def normal_values(rng, dims, deviation, reach, cuts=(), kind=jnp.bfloat16):
    values = jax.random.normal(rng, dims, jnp.float32) * deviation
    if len(cuts) > 0:
        values = levels(rng, dims, cuts, -0.22, 0.18) * values
    return jnp.clip(values, min=-reach, max=reach).astype(kind)


def setup_inputs(seed: int = 0) -> dict:
    key_of = jax.random.split(jax.random.key(seed), 6)
    samples = draw_samples(jax.random.fold_in(key_of[5], 71), 0)
    estimate = normal_values(key_of[1], (NB, KMAX * BLK, BLK), 1.0, 6.0, ((0, 4),), jnp.float32)
    block_rows = draw_block_rows(jax.random.fold_in(key_of[5], 71), 0)
    counts = draw_counts(jax.random.fold_in(key_of[5], 71), 0)
    holder = jax.random.permutation(key_of[4], NB).astype(jnp.int32)
    return dict(samples=samples, estimate=estimate, block_rows=block_rows, counts=counts, holder=holder)


step_size = 0.1
penalty = 5.0

def proximal(current, gradient, diag_flag, live_flag):
    stepped = current - step_size * gradient
    shrunk = jnp.sign(stepped) * jnp.maximum(jnp.abs(stepped) - step_size * penalty, 0.0)
    barrier = 0.5 * (stepped + jnp.sqrt(stepped * stepped + 4.0 * step_size))
    return jnp.where(live_flag, jnp.where(diag_flag, barrier, shrunk), 0.0)

def reference(samples, estimate, block_rows, counts, holder):
    slot_count = estimate.shape[1] // BLK
    sample_total = samples.shape[0]
    columns = holder
    rows_of = block_rows[columns]
    live_mask = jnp.arange(slot_count, dtype=jnp.int32)[None, :] < counts[columns][:, None]
    position = jnp.argsort(holder).astype(jnp.int32)
    same_entry = jnp.arange(BLK)[:, None] == jnp.arange(BLK)[None, :]
    diag_flag = ((rows_of == columns[:, None])[:, :, None, None] & same_entry[None, None]).reshape(NB, slot_count * BLK, BLK)
    live_flag = jnp.broadcast_to(live_mask[:, :, None, None], (NB, slot_count, BLK, BLK)).reshape(NB, slot_count * BLK, BLK)
    precision = estimate
    for iteration in range(ITERS):
        weights = jnp.where(live_mask[:, :, None, None], precision.reshape(NB, slot_count, BLK, BLK), 0.0).astype(jnp.bfloat16)

        def project(stored):
            picked = jnp.take(samples, rows_of[stored], axis=1).astype(jnp.float32)
            return jnp.einsum('nsa,sab->nb', picked, weights[stored].astype(jnp.float32)).astype(jnp.bfloat16)
        projected = lax.map(project, jnp.arange(NB, dtype=jnp.int32))

        def gram_block(stored):
            picked = jnp.take(samples, rows_of[stored], axis=1).astype(jnp.float32)
            mirror = jnp.take(projected, position[rows_of[stored]], axis=0).astype(jnp.float32)
            own_blocks = jnp.take(samples, columns[stored], axis=1).astype(jnp.float32)
            own_proj = projected[stored].astype(jnp.float32)
            return jnp.einsum('nsa,nb->sab', picked, own_proj) + jnp.einsum('sna,nb->sab', mirror, own_blocks)
        gram_terms = lax.map(gram_block, jnp.arange(NB, dtype=jnp.int32))
        gradient = gram_terms.reshape(NB, slot_count * BLK, BLK) / (2.0 * sample_total)
        precision = proximal(precision, gradient, diag_flag, live_flag)
    return precision
```

```python
import functools

import jax
import jax.numpy as jnp
from jax import lax
from jax.experimental import pallas as pl
from jax.experimental.pallas import tpu as pltpu
from jax.sharding import PartitionSpec as P

MESH = pl.DeviceIdType.MESH
ITERS = 2
PAIRS = 24
step_size = 0.1
penalty = 5.0


def exchange_kernel(
    dims, sample_total, sa, sb, own_ref, est_ref, cov_ref, all_ref,
    data, part, twin, acc, got1, mid, got2, share,
    x_send, x_recv, d_send, d_recv, s1_send, s1_recv, s2_send, s2_recv,
    e_send, e_recv, b_send, b_recv, r_send, r_recv, l_send, l_recv,
    t_send, t_recv, p_send, p_recv, pd_send, pd_recv, loc_sem,
):
    nx, ny, nz = dims
    s = lax.axis_index("samp")
    x = lax.axis_index("var")
    c = lax.rem(s, 2)
    z = lax.rem(s // 2, nz)
    y = s // (2 * nz)
    own_blocks = own_ref.shape[0]
    per_x = PAIRS // nx
    rows = acc.shape[0]
    half = rows // per_x

    def at(xx, yy, zz, cc):
        return ((yy * nz + zz) * 2 + cc, xx)

    def x_peer(k):
        return at(lax.rem(x + k, nx), y, z, c)

    def y_peer(k):
        return at(x, lax.rem(y + k, ny), z, c)

    def z_peer(k):
        return at(x, y, lax.rem(z + k, nz), c)

    sibling = at(x, y, z, 1 - c)

    def copy(src, dst, send, recv, device):
        return pltpu.make_async_remote_copy(
            src_ref=src, dst_ref=dst, send_sem=send, recv_sem=recv, device_id=device, device_id_type=MESH
        )

    barrier = pltpu.get_barrier_semaphore()
    for peer, n in ((x_peer, nx), (y_peer, ny), (z_peer, nz)):
        @pl.loop(1, n)
        def _(k, peer=peer):
            pl.semaphore_signal(barrier, inc=1, device_id=peer(k), device_id_type=MESH)
    pl.semaphore_signal(barrier, inc=1, device_id=sibling, device_id_type=MESH)
    pl.semaphore_wait(barrier, nx + ny + nz - 2)

    mine = pl.ds(x * own_blocks, own_blocks)
    x_copies = [copy(own_ref, data.at[mine], x_send.at[k - 1], x_recv.at[k - 1], x_peer(k)) for k in range(1, nx)]
    for cp in x_copies:
        cp.start()
    est_local = pltpu.make_async_copy(est_ref, all_ref.at[mine], loc_sem)
    est_local.start()
    data[mine] = own_ref[...]
    for cp in x_copies:
        cp.wait()

    est_copies = [
        copy(est_ref.at[pl.ds(c * (own_blocks // 2), own_blocks // 2)],
             all_ref.at[pl.ds(x * own_blocks + c * (own_blocks // 2), own_blocks // 2)],
             p_send.at[k - 1], p_recv.at[k - 1], x_peer(k))
        for k in range(1, nx)
    ]
    for cp in est_copies:
        cp.start()

    pair_copies = []
    for u in range(per_x):
        left = data[sa[x * per_x + u]]
        right = data[sb[x * per_x + u]]
        prod = lax.dot_general(left, right, (((0,), (0,)), ((), ())), preferred_element_type=jnp.float32)
        part[0, u] = prod[:half]
        part[1, u] = prod[half:]
        cp = copy(part.at[1 - c, u], twin.at[u], d_send.at[u], d_recv.at[u], sibling)
        cp.start()
        pair_copies.append(cp)
    for u in range(per_x):
        pair_copies[u].wait()
        acc[u * half:(u + 1) * half] = part[c, u] + twin[u]

    def reduce_and_gather(me_a, peer_a, n_a, me_b, peer_b, n_b, other_rows, other_n):
        rows_a = rows // n_a
        rows_b = rows_a // n_b

        def first(k):
            return copy(
                acc.at[pl.ds(lax.rem(me_a + k, n_a) * rows_a, rows_a)], got1.at[k - 1, pl.ds(0, rows_a)],
                s1_send.at[k - 1], s1_recv.at[k - 1], peer_a(k),
            )

        @pl.loop(1, n_a)
        def _(k):
            first(k).start()

        mid[pl.ds(0, rows_a)] = acc[pl.ds(pl.multiple_of(me_a * rows_a, 8), rows_a)]

        @pl.loop(1, n_a)
        def _(k):
            first(k).wait()
            mid[pl.ds(0, rows_a)] += got1[k - 1, pl.ds(0, rows_a)]

        def second(k):
            return copy(
                mid.at[pl.ds(lax.rem(me_b + k, n_b) * rows_b, rows_b)], got2.at[k - 1],
                s2_send.at[k - 1], s2_recv.at[k - 1], peer_b(k),
            )

        @pl.loop(1, n_b)
        def _(k):
            second(k).start()

        share[...] = mid[pl.ds(pl.multiple_of(me_b * rows_b, 8), rows_b)]

        @pl.loop(1, n_b)
        def _(k):
            second(k).wait()
            share[...] += got2[k - 1]

        share[...] = share[...] * (1.0 / sample_total)

        first_row = pl.multiple_of(me_a * rows_a + me_b * rows_b, 8)
        place = pl.ds(first_row, rows_b)

        def third(k):
            return copy(share, cov_ref.at[x, c, place], e_send.at[k - 1], e_recv.at[k - 1], x_peer(k))

        @pl.loop(1, nx)
        def _(k):
            third(k).start()

        cov_ref[x, c, place] = share[...]

        @pl.loop(1, nx)
        def _(k):
            third(k).wait()

        def fourth(k):
            ref = cov_ref.at[:, c, place]
            return copy(ref, ref, b_send.at[k - 1], b_recv.at[k - 1], peer_b(k))

        @pl.loop(1, n_b)
        def _(k):
            fourth(k).start()

        @pl.loop(1, n_b)
        def _(k):
            fourth(k).wait()

        def chunk(owner):
            return cov_ref.at[:, c, pl.ds(pl.multiple_of(owner * rows_a, 8), rows_a)]

        rights, lefts = n_a // 2, n_a - 1 - n_a // 2

        def to_right(t):
            ref = chunk(lax.rem(me_a - t + n_a, n_a))
            return copy(ref, ref, r_send.at[t], r_recv.at[t], peer_a(1))

        def to_left(t):
            ref = chunk(lax.rem(me_a + t, n_a))
            return copy(ref, ref, l_send.at[t], l_recv.at[t], peer_a(n_a - 1))

        def to_twin(owner):
            ref = chunk(owner)
            return copy(ref, ref, t_send.at[owner], t_recv.at[owner], sibling)

        for t in range(rights):
            to_right(t).start()
            if t < lefts:
                to_left(t).start()
            if t == 0:
                to_twin(me_a).start()
            else:
                to_twin(lax.rem(me_a - t + n_a, n_a)).start()
                if t - 1 < lefts:
                    to_twin(lax.rem(me_a + t, n_a)).start()
            to_right(t).wait()
            if t < lefts:
                to_left(t).wait()
        to_twin(lax.rem(me_a - rights + n_a, n_a)).start()
        if lefts == rights:
            to_twin(lax.rem(me_a + lefts, n_a)).start()

        @pl.loop(0, other_n)
        def _(owner):
            ref = cov_ref.at[:, 1 - c, pl.ds(pl.multiple_of(owner * other_rows, 8), other_rows)]
            copy(ref, ref, t_send.at[owner], t_recv.at[owner], sibling).wait_recv()

        @pl.loop(0, n_a)
        def _(owner):
            to_twin(owner).wait_send()

    @pl.when(c == 0)
    def _():
        reduce_and_gather(y, y_peer, ny, z, z_peer, nz, rows // nz, nz)

    @pl.when(c == 1)
    def _():
        reduce_and_gather(z, z_peer, nz, y, y_peer, ny, rows // ny, ny)

    for cp in est_copies:
        cp.wait()
    est_local.wait()

    def est_twin(k):
        ref = all_ref.at[pl.ds(lax.rem(x + k, nx) * own_blocks + c * (own_blocks // 2), own_blocks // 2)]
        return copy(ref, ref, pd_send.at[k - 1], pd_recv.at[k - 1], sibling)

    for k in range(1, nx):
        est_twin(k).start()
    for k in range(1, nx):
        est_twin(k).wait()


def exchange(dims, sample_total, sa, sb, own, estimate):
    nx, ny, nz = dims
    own_blocks, rows_dev, width = own.shape
    blocks = own_blocks * nx
    per_x = PAIRS // nx
    half = width // 2
    rows = per_x * half
    most = max(ny, nz)
    dma = pltpu.SemaphoreType.DMA
    f32 = jnp.float32
    smem = pl.BlockSpec(memory_space=pltpu.SMEM)
    vmem = pl.BlockSpec(memory_space=pltpu.VMEM)
    hbm = pl.BlockSpec(memory_space=pl.ANY)
    return pl.pallas_call(
        functools.partial(exchange_kernel, dims, sample_total),
        out_shape=(
            jax.ShapeDtypeStruct((nx, 2, rows, width), f32),
            jax.ShapeDtypeStruct((blocks,) + estimate.shape[1:], f32),
        ),
        in_specs=[smem, smem, vmem, hbm],
        out_specs=(vmem, hbm),
        scratch_shapes=[
            pltpu.VMEM((blocks, rows_dev, width), jnp.bfloat16),
            pltpu.VMEM((2, per_x, half, width), f32),
            pltpu.VMEM((per_x, half, width), f32),
            pltpu.VMEM((rows, width), f32),
            pltpu.VMEM((most - 1, rows // min(ny, nz), width), f32),
            pltpu.VMEM((rows // min(ny, nz), width), f32),
            pltpu.VMEM((most - 1, rows // (ny * nz), width), f32),
            pltpu.VMEM((rows // (ny * nz), width), f32),
            dma((nx - 1,)), dma((nx - 1,)),
            dma((per_x,)), dma((per_x,)),
            dma((most - 1,)), dma((most - 1,)),
            dma((most - 1,)), dma((most - 1,)),
            dma((nx - 1,)), dma((nx - 1,)),
            dma((most - 1,)), dma((most - 1,)),
            dma((most,)), dma((most,)),
            dma((most,)), dma((most,)),
            dma((most,)), dma((most,)),
            dma((nx - 1,)), dma((nx - 1,)),
            dma((nx - 1,)), dma((nx - 1,)),
            dma,
        ],
        compiler_params=pltpu.CompilerParams(
            collective_id=0, has_side_effects=True, vmem_limit_bytes=48 << 20
        ),
    )(sa, sb, own, estimate)


def steps_kernel(
    nx, holder, table, counts, position, slot_of_pair, place, cov_ref, est_ref, out_ref,
    high, low, prec, weights, turned, terms,
):
    blocks = holder.shape[0]
    slots = table.shape[1]
    width = est_ref.shape[-1]
    half = width // 2
    per_x = PAIRS // nx
    f32, bf16 = jnp.float32, jnp.bfloat16

    @pl.loop(0, PAIRS)
    def _(t):
        u = lax.rem(t, per_x)
        for h in range(2):
            value = cov_ref[t // per_x, h, pl.ds(pl.multiple_of(u * half, 8), half)]
            top = value.astype(bf16)
            high[t, h * half:(h + 1) * half] = top
            low[t, h * half:(h + 1) * half] = (value - top.astype(f32)).astype(bf16)

    def set_weights(flat, value):
        rounded = value.astype(bf16)
        weights[flat] = rounded
        turned[flat] = rounded.T

    def block_of(q, s):
        return est_ref[q, pl.ds(pl.multiple_of(s * width, 8), width)]

    def mirror(j, i):
        return jnp.where(table[i, 0] == j, 0, jnp.where(table[i, 1] == j, 1, 2))

    @pl.loop(0, blocks * slots)
    def _(flat):
        q, s = flat // slots, lax.rem(flat, slots)

        @pl.when(s < counts[holder[q]])
        def _():
            value = block_of(q, s)
            prec[flat] = value
            set_weights(flat, value)

    def term(q, s):
        j = holder[q]
        i = table[j, s]
        qi = position[i]
        dest = q * slots + s
        terms[dest] = jnp.zeros((width, width), f32)
        for t in range(slots):
            r = table[j, t]

            @pl.when((t < counts[j]) & (i <= r))
            def _():
                pair = slot_of_pair[i * blocks + r]
                w = weights[q * slots + t]
                terms[dest] += jnp.dot(high[pair], w, preferred_element_type=f32) + jnp.dot(
                    low[pair], w, preferred_element_type=f32
                )
        for t in range(slots):
            r = table[i, t]

            @pl.when((t < counts[i]) & (r < j))
            def _():
                pair = slot_of_pair[r * blocks + j]
                w = turned[qi * slots + t]
                terms[dest] += jnp.dot(w, high[pair], preferred_element_type=f32) + jnp.dot(
                    w, low[pair], preferred_element_type=f32
                )

    def update(q, s):
        j = holder[q]
        i = table[j, s]
        other = position[i] * slots + mirror(j, i)
        gram = terms[q * slots + s] + terms[other].T
        stepped = prec[q * slots + s] - (0.5 * step_size) * gram
        bound = step_size * penalty
        shrunk = jnp.maximum(stepped - bound, 0.0) + jnp.minimum(stepped + bound, 0.0)
        barrier = 0.5 * (stepped + jnp.sqrt(stepped * stepped + 4.0 * step_size))
        same = lax.broadcasted_iota(jnp.int32, (width, width), 0) == lax.broadcasted_iota(
            jnp.int32, (width, width), 1
        )
        return jnp.where(same & (i == j), barrier, shrunk)

    for _ in range(ITERS - 1):
        @pl.loop(0, blocks * slots)
        def _(flat):
            q, s = flat // slots, lax.rem(flat, slots)

            @pl.when(s < counts[holder[q]])
            def _():
                term(q, s)

        @pl.loop(0, blocks * slots)
        def _(flat):
            q, s = flat // slots, lax.rem(flat, slots)

            @pl.when(s < counts[holder[q]])
            def _():
                value = update(q, s)
                prec[flat] = value
                set_weights(flat, value)

    own_count, own_rows = out_ref.shape[0], out_ref.shape[1]
    s = place[1]
    first_row = place[2]
    for n in range(own_count):
        q = place[0] * own_count + n
        j = holder[q]
        live = s < counts[j]

        @pl.when(live)
        def _():
            i = table[j, s]
            term(q, s)

            @pl.when(i != j)
            def _():
                term(position[i], mirror(j, i))

            high_rows = update(q, s)
            terms[0] = high_rows
            if own_rows % 8 == 0:
                out_ref[n] = terms[0, pl.ds(pl.multiple_of(first_row, 8), own_rows)]
            else:
                eight = terms[0, pl.ds(pl.multiple_of(first_row // 8 * 8, 8), 8)]
                out_ref[n] = jnp.where(lax.rem(first_row, 8) == 0, eight[:own_rows], eight[8 - own_rows:])

        @pl.when(jnp.logical_not(live))
        def _():
            out_ref[n] = jnp.zeros(out_ref.shape[1:], f32)


def steps(nx, holder, table, counts, position, slot_of_pair, place, cov, estimate, own_rows):
    blocks, _, width = estimate.shape
    slots = table.shape[1]
    f32, bf16 = jnp.float32, jnp.bfloat16
    vmem = pl.BlockSpec(memory_space=pltpu.VMEM)
    smem = pl.BlockSpec(memory_space=pltpu.SMEM)
    return pl.pallas_call(
        functools.partial(steps_kernel, nx),
        out_shape=jax.ShapeDtypeStruct((blocks // nx, own_rows, width), f32),
        in_specs=[smem] * 6 + [vmem] * 2,
        out_specs=vmem,
        scratch_shapes=[
            pltpu.VMEM((PAIRS, width, width), bf16),
            pltpu.VMEM((PAIRS, width, width), bf16),
            pltpu.VMEM((blocks * slots, width, width), f32),
            pltpu.VMEM((blocks * slots, width, width), bf16),
            pltpu.VMEM((blocks * slots, width, width), bf16),
            pltpu.VMEM((blocks * slots, width, width), f32),
        ],
        compiler_params=pltpu.CompilerParams(vmem_limit_bytes=52 << 20),
    )(holder, table, counts, position, slot_of_pair, place, cov, estimate)


def pair_tables(block_rows, counts):
    blocks, slots = block_rows.shape
    ids = jnp.arange(blocks, dtype=jnp.int32)
    live = jnp.arange(slots, dtype=jnp.int32)[None, :] < counts[:, None]
    has = jnp.any(live[:, :, None] & (block_rows[:, :, None] == ids), axis=1)
    need = jnp.any(has[:, :, None] & has[:, None, :], axis=0) & (ids[:, None] <= ids[None, :])
    flat = need.reshape(-1).astype(jnp.int32)
    order = jnp.arange(blocks * blocks, dtype=jnp.int32)
    rank = jnp.sum(jnp.where(order[None, :] < order[:, None], flat[None, :], 0), axis=1)
    hit = (flat[None, :] > 0) & (rank[None, :] == jnp.arange(PAIRS, dtype=jnp.int32)[:, None])
    which = jnp.sum(jnp.where(hit, order[None, :], 0), axis=1)
    return which // blocks, which % blocks, rank


def body(dims, samples, estimate, block_rows, counts, holder):
    nx, ny, nz = dims
    rows_dev, own_blocks, width = samples.shape
    samp_count = 2 * ny * nz
    blocks = holder.shape[0]
    slots = block_rows.shape[1]
    sa, sb, rank = pair_tables(block_rows, counts)
    ids = jnp.arange(blocks, dtype=jnp.int32)
    position = jnp.sum(jnp.where(holder[:, None] == ids[None, :], ids[:, None], 0), axis=0)
    own_rows = slots * width // samp_count
    first = lax.axis_index("samp") * own_rows
    place = jnp.stack([lax.axis_index("var"), first // width, first % width]).astype(jnp.int32)
    own = samples.transpose(1, 0, 2)
    cov, every = exchange(dims, rows_dev * samp_count, sa, sb, own, estimate)
    return steps(nx, holder, block_rows, counts, position, rank, place, cov, every, own_rows)


def solution(mesh):
    nx = mesh.shape["var"]
    ny, nz = (8, 12) if mesh.shape["samp"] == 192 else (2, 3)
    return jax.shard_map(
        functools.partial(body, (nx, ny, nz)),
        mesh=mesh,
        in_specs=(P("samp", "var", None), P("var", None, None), P(), P(), P()),
        out_specs=P("var", "samp", None),
        check_vma=False,
    )
```

```python
import functools

import jax
import jax.numpy as jnp
from jax import lax
from jax.experimental import pallas as pl
from jax.experimental.pallas import tpu as pltpu
from jax.sharding import PartitionSpec as P

MESH = pl.DeviceIdType.MESH
ITERS = 2
PAIRS = 24
VMEM_EXCHANGE = 12 << 20
VMEM_STEPS = 34 << 20

TABLE, COUNTS, HOLDER, POSITION, RANK, LEFT, RIGHT, PLACE = 0, 24, 32, 40, 48, 112, 136, 160
step_size = 0.1
penalty = 5.0


def exchange_kernel(
    dims, sample_total, tab, own_ref, est_ref, cov_ref, all_ref,
    data, part, twin, acc, got1, mid, got2, share,
    x_send, x_recv, d_send, d_recv, s1_send, s1_recv, s2_send, s2_recv,
    e_send, e_recv, b_send, b_recv, r_send, r_recv, l_send, l_recv,
    t_send, t_recv, p_send, p_recv, pd_send, pd_recv, loc_sem,
):
    nx, ny, nz = dims
    s = lax.axis_index("samp")
    x = lax.axis_index("var")
    c = lax.rem(s, 2)
    z = lax.rem(s // 2, nz)
    y = s // (2 * nz)
    own_blocks = own_ref.shape[0]
    per_x = PAIRS // nx
    rows = acc.shape[0]
    half = rows // per_x

    def at(xx, yy, zz, cc):
        return ((yy * nz + zz) * 2 + cc, xx)

    def x_peer(k):
        return at(lax.rem(x + k, nx), y, z, c)

    def y_peer(k):
        return at(x, lax.rem(y + k, ny), z, c)

    def z_peer(k):
        return at(x, y, lax.rem(z + k, nz), c)

    sibling = at(x, y, z, 1 - c)

    def copy(src, dst, send, recv, device):
        return pltpu.make_async_remote_copy(
            src_ref=src, dst_ref=dst, send_sem=send, recv_sem=recv, device_id=device, device_id_type=MESH
        )

    barrier = pltpu.get_barrier_semaphore()
    for peer, n in ((x_peer, nx), (y_peer, ny), (z_peer, nz)):
        @pl.loop(1, n)
        def _(k, peer=peer):
            pl.semaphore_signal(barrier, inc=1, device_id=peer(k), device_id_type=MESH)
    pl.semaphore_signal(barrier, inc=1, device_id=sibling, device_id_type=MESH)
    pl.semaphore_wait(barrier, nx + ny + nz - 2)

    class Ring:
        def __init__(self, own_piece, piece, send, recv):
            right, left = lax.rem(x + 1, nx), lax.rem(x + nx - 1, nx)

            def to(k, owner, n, sem):
                src = own_piece(n) if owner is None else piece(owner, n)
                dst = piece(x if owner is None else owner, n)
                return copy(src, dst, send.at[sem], recv.at[sem], x_peer(k))

            self.own = [to(1, None, 0, 0), to(nx - 1, None, 1, 1), to(1, None, 1, 2), to(nx - 1, None, 0, 3)]
            self.onward = [to(1, left, 0, 4), to(nx - 1, right, 1, 5)]

        def start(self):
            for cp in self.own:
                cp.start()

        def forward(self):
            for n in range(2):
                self.own[n].wait_recv()
                self.onward[n].start()

        def finish(self):
            self.own[2].wait_recv()
            self.own[3].wait_recv()
            for cp in self.onward:
                cp.wait_recv()
            for cp in self.own + self.onward:
                cp.wait_send()

    mine = pl.ds(x * own_blocks, own_blocks)
    samples_ring = Ring(
        lambda n: own_ref.at[n], lambda owner, n: data.at[owner * own_blocks + n], x_send, x_recv
    )
    samples_ring.start()
    est_local = pltpu.make_async_copy(est_ref, all_ref.at[mine], loc_sem.at[0])
    est_local.start()
    data[mine] = own_ref[...]
    samples_ring.forward()
    samples_ring.finish()

    est_half = est_ref.shape[1] // 2

    def est_rows(n):
        return pl.ds(n * est_half, est_half)

    est_ring = Ring(
        lambda n: est_ref.at[c, est_rows(n)],
        lambda owner, n: all_ref.at[owner * own_blocks + c, est_rows(n)],
        p_send, p_recv,
    )
    est_ring.start()

    pair_copies = []
    for u in range(per_x):
        left = data[tab[LEFT + x * per_x + u]]
        right = data[tab[RIGHT + x * per_x + u]]
        prod = lax.dot_general(left, right, (((0,), (0,)), ((), ())), preferred_element_type=jnp.float32)
        part[0, u] = prod[:half]
        part[1, u] = prod[half:]
        cp = copy(part.at[1 - c, u], twin.at[u], d_send.at[u], d_recv.at[u], sibling)
        cp.start()
        pair_copies.append(cp)
    for u in range(per_x):
        pair_copies[u].wait()
        acc[u * half:(u + 1) * half] = part[c, u] + twin[u]

    def est_twin(k):
        ref = all_ref.at[lax.rem(x + k, nx) * own_blocks + c]
        return copy(ref, ref, pd_send.at[k - 1], pd_recv.at[k - 1], sibling)

    def reduce_and_gather(me_a, peer_a, n_a, me_b, peer_b, n_b, other_rows, other_n):
        rows_a = rows // n_a
        rows_b = rows_a // n_b

        def first(k):
            return copy(
                acc.at[pl.ds(lax.rem(me_a + k, n_a) * rows_a, rows_a)], got1.at[k - 1, pl.ds(0, rows_a)],
                s1_send.at[k - 1], s1_recv.at[k - 1], peer_a(k),
            )

        @pl.loop(1, n_a)
        def _(k):
            first(k).start()

        mid[pl.ds(0, rows_a)] = acc[pl.ds(pl.multiple_of(me_a * rows_a, 8), rows_a)]

        @pl.loop(1, n_a)
        def _(k):
            first(k).wait()
            mid[pl.ds(0, rows_a)] += got1[k - 1, pl.ds(0, rows_a)]

        def second(k):
            return copy(
                mid.at[pl.ds(lax.rem(me_b + k, n_b) * rows_b, rows_b)], got2.at[k - 1],
                s2_send.at[k - 1], s2_recv.at[k - 1], peer_b(k),
            )

        @pl.loop(1, n_b)
        def _(k):
            second(k).start()

        est_ring.forward()
        share[...] = mid[pl.ds(pl.multiple_of(me_b * rows_b, 8), rows_b)]

        @pl.loop(1, n_b)
        def _(k):
            second(k).wait()
            share[...] += got2[k - 1]

        share[...] = share[...] * (1.0 / sample_total)

        first_row = pl.multiple_of(me_a * rows_a + me_b * rows_b, 8)
        place = pl.ds(first_row, rows_b)

        def third(k):
            return copy(share, cov_ref.at[x, c, place], e_send.at[k - 1], e_recv.at[k - 1], x_peer(k))

        @pl.loop(1, nx)
        def _(k):
            third(k).start()

        own_share = pltpu.make_async_copy(share, cov_ref.at[x, c, place], loc_sem.at[1])
        own_share.start()
        own_share.wait()

        @pl.loop(1, nx)
        def _(k):
            third(k).wait()

        def fourth(k):
            ref = cov_ref.at[:, c, place]
            return copy(ref, ref, b_send.at[k - 1], b_recv.at[k - 1], peer_b(k))

        @pl.loop(1, n_b)
        def _(k):
            fourth(k).start()

        est_ring.finish()
        for k in range(1, nx):
            est_twin(k).start()

        @pl.loop(1, n_b)
        def _(k):
            fourth(k).wait()

        part_x = nx // 2

        def chunk(owner, h):
            return cov_ref.at[
                pl.ds(h * part_x, part_x), c, pl.ds(pl.multiple_of(owner * rows_a, 8), rows_a)
            ]

        def ahead(t):
            return lax.rem(me_a + t, n_a)

        def behind(t):
            return lax.rem(me_a - t + n_a, n_a)

        def to_right(t, h):
            ref = chunk(behind(t), h)
            return copy(ref, ref, r_send.at[2 * t + h], r_recv.at[2 * t + h], peer_a(1))

        def to_left(t, h):
            ref = chunk(ahead(t), h)
            return copy(ref, ref, l_send.at[2 * t + h], l_recv.at[2 * t + h], peer_a(n_a - 1))

        def to_twin(owner, h):
            ref = chunk(owner, h)
            return copy(ref, ref, t_send.at[2 * owner + h], t_recv.at[2 * owner + h], sibling)

        whole = (n_a - 1) // 2
        right_steps = [(t, h) for t in range(whole) for h in range(2)]
        left_steps = list(right_steps)
        if n_a % 2 == 0:
            right_steps.append((whole, 0))
            left_steps.append((whole, 1))
        for t in range(whole + 1):
            for h in range(2):
                if (t, h) in right_steps:
                    if t > 0:
                        to_right(t - 1, h).wait_recv()
                    to_right(t, h).start()
                    if t > 0:
                        to_twin(behind(t), h).start()
                if (t, h) in left_steps:
                    if t > 0:
                        to_left(t - 1, h).wait_recv()
                    to_left(t, h).start()
                    if t > 0:
                        to_twin(ahead(t), h).start()
            if t == 0:
                to_twin(me_a, 0).start()
                to_twin(me_a, 1).start()
        for t, h in right_steps:
            if (t + 1, h) not in right_steps:
                to_right(t, h).wait_recv()
                to_twin(behind(t + 1), h).start()
        for t, h in left_steps:
            if (t + 1, h) not in left_steps:
                to_left(t, h).wait_recv()
                to_twin(ahead(t + 1), h).start()
        for t, h in right_steps:
            to_right(t, h).wait_send()
        for t, h in left_steps:
            to_left(t, h).wait_send()

        @pl.loop(0, 2 * other_n)
        def _(n):
            ref = cov_ref.at[
                pl.ds(lax.rem(n, 2) * part_x, part_x), 1 - c,
                pl.ds(pl.multiple_of(n // 2 * other_rows, 8), other_rows),
            ]
            copy(ref, ref, t_send.at[n], t_recv.at[n], sibling).wait_recv()

        @pl.loop(0, 2 * n_a)
        def _(n):
            to_twin(n // 2, lax.rem(n, 2)).wait_send()

    @pl.when(c == 0)
    def _():
        reduce_and_gather(y, y_peer, ny, z, z_peer, nz, rows // nz, nz)

    @pl.when(c == 1)
    def _():
        reduce_and_gather(z, z_peer, nz, y, y_peer, ny, rows // ny, ny)

    est_local.wait()
    for k in range(1, nx):
        est_twin(k).wait()


def exchange(dims, sample_total, tab, own, estimate):
    nx, ny, nz = dims
    own_blocks, rows_dev, width = own.shape
    blocks = own_blocks * nx
    per_x = PAIRS // nx
    half = width // 2
    rows = per_x * half
    most = max(ny, nz)
    dma = pltpu.SemaphoreType.DMA
    f32 = jnp.float32
    smem = pl.BlockSpec(memory_space=pltpu.SMEM)
    vmem = pl.BlockSpec(memory_space=pltpu.VMEM)
    hbm = pl.BlockSpec(memory_space=pl.ANY)
    return pl.pallas_call(
        functools.partial(exchange_kernel, dims, sample_total),
        out_shape=(
            jax.ShapeDtypeStruct((nx, 2, rows, width), f32),
            jax.ShapeDtypeStruct((blocks,) + estimate.shape[1:], f32),
        ),
        in_specs=[smem, vmem, hbm],
        out_specs=(hbm, hbm),
        scratch_shapes=[
            pltpu.VMEM((blocks, rows_dev, width), jnp.bfloat16),
            pltpu.VMEM((2, per_x, half, width), f32),
            pltpu.VMEM((per_x, half, width), f32),
            pltpu.VMEM((rows, width), f32),
            pltpu.VMEM((most - 1, rows // min(ny, nz), width), f32),
            pltpu.VMEM((rows // min(ny, nz), width), f32),
            pltpu.VMEM((most - 1, rows // (ny * nz), width), f32),
            pltpu.VMEM((rows // (ny * nz), width), f32),
            dma((6,)), dma((6,)),
            dma((per_x,)), dma((per_x,)),
            dma((most - 1,)), dma((most - 1,)),
            dma((most - 1,)), dma((most - 1,)),
            dma((nx - 1,)), dma((nx - 1,)),
            dma((most - 1,)), dma((most - 1,)),
            dma((2 * most,)), dma((2 * most,)),
            dma((2 * most,)), dma((2 * most,)),
            dma((2 * most,)), dma((2 * most,)),
            dma((6,)), dma((6,)),
            dma((nx - 1,)), dma((nx - 1,)),
            dma((2,)),
        ],
        compiler_params=pltpu.CompilerParams(
            collective_id=0, has_side_effects=True, vmem_limit_bytes=VMEM_EXCHANGE
        ),
    )(tab, own, estimate)


def steps_kernel(
    nx, tab, cov_ref, est_ref, out_ref,
    high, low, prec, weights, turned, terms,
):
    blocks, stacked, width = est_ref.shape
    slots = stacked // width
    half = width // 2
    per_x = PAIRS // nx
    f32, bf16 = jnp.float32, jnp.bfloat16

    @pl.loop(0, PAIRS)
    def _(t):
        u = lax.rem(t, per_x)
        for h in range(2):
            value = cov_ref[t // per_x, h, pl.ds(pl.multiple_of(u * half, 8), half)]
            top = value.astype(bf16)
            high[t, h * half:(h + 1) * half] = top
            low[t, h * half:(h + 1) * half] = (value - top.astype(f32)).astype(bf16)

    def row_of(j, s):
        return tab[TABLE + j * slots + s]

    def count(j):
        return tab[COUNTS + j]

    def holder(q):
        return tab[HOLDER + q]

    def position(i):
        return tab[POSITION + i]

    def pair_of(a, b):
        return tab[RANK + a * blocks + b]

    def set_weights(flat, value):
        rounded = value.astype(bf16)
        weights[flat] = rounded
        turned[flat] = rounded.T

    def block_of(q, s):
        return est_ref[q, pl.ds(pl.multiple_of(s * width, 8), width)]

    def mirror(j, i):
        return jnp.where(row_of(i, 0) == j, 0, jnp.where(row_of(i, 1) == j, 1, 2))

    @pl.loop(0, blocks * slots)
    def _(flat):
        q, s = flat // slots, lax.rem(flat, slots)

        @pl.when(s < count(holder(q)))
        def _():
            set_weights(flat, block_of(q, s))

    def term(q, s):
        j = holder(q)
        i = row_of(j, s)
        qi = position(i)
        dest = q * slots + s
        terms[dest] = jnp.zeros((width, width), f32)
        for t in range(slots):
            r = row_of(j, t)

            @pl.when((t < count(j)) & (i <= r))
            def _():
                pair = pair_of(i, r)
                w = weights[q * slots + t]
                terms[dest] += jnp.dot(high[pair], w, preferred_element_type=f32) + jnp.dot(
                    low[pair], w, preferred_element_type=f32
                )
        for t in range(slots):
            r = row_of(i, t)

            @pl.when((t < count(i)) & (r < j))
            def _():
                pair = pair_of(r, j)
                w = turned[qi * slots + t]
                terms[dest] += jnp.dot(w, high[pair], preferred_element_type=f32) + jnp.dot(
                    w, low[pair], preferred_element_type=f32
                )

    def update(q, s, current):
        j = holder(q)
        i = row_of(j, s)
        other = position(i) * slots + mirror(j, i)
        gram = terms[q * slots + s] + terms[other].T
        stepped = current - (0.5 * step_size) * gram
        bound = step_size * penalty
        shrunk = jnp.maximum(stepped - bound, 0.0) + jnp.minimum(stepped + bound, 0.0)
        barrier = 0.5 * (stepped + jnp.sqrt(stepped * stepped + 4.0 * step_size))
        same = lax.broadcasted_iota(jnp.int32, (width, width), 0) == lax.broadcasted_iota(
            jnp.int32, (width, width), 1
        )
        return jnp.where(same & (i == j), barrier, shrunk)

    for iteration in range(ITERS - 1):
        @pl.loop(0, blocks * slots)
        def _(flat):
            q, s = flat // slots, lax.rem(flat, slots)

            @pl.when(s < count(holder(q)))
            def _():
                term(q, s)

        @pl.loop(0, blocks * slots)
        def _(flat):
            q, s = flat // slots, lax.rem(flat, slots)

            @pl.when(s < count(holder(q)))
            def _():
                value = update(q, s, block_of(q, s) if iteration == 0 else prec[flat])
                prec[flat] = value
                set_weights(flat, value)

    own_count, own_rows = out_ref.shape[0], out_ref.shape[1]
    s = tab[PLACE + 1]
    first_row = tab[PLACE + 2]
    for n in range(own_count):
        q = tab[PLACE] * own_count + n
        j = holder(q)
        live = s < count(j)

        @pl.when(live)
        def _():
            i = row_of(j, s)
            term(q, s)

            @pl.when(i != j)
            def _():
                term(position(i), mirror(j, i))

            terms[0] = update(q, s, prec[q * slots + s])
            if own_rows % 8 == 0:
                out_ref[n] = terms[0, pl.ds(pl.multiple_of(first_row, 8), own_rows)]
            else:
                eight = terms[0, pl.ds(pl.multiple_of(first_row // 8 * 8, 8), 8)]
                out_ref[n] = jnp.where(lax.rem(first_row, 8) == 0, eight[:own_rows], eight[8 - own_rows:])

        @pl.when(jnp.logical_not(live))
        def _():
            out_ref[n] = jnp.zeros(out_ref.shape[1:], f32)


def steps(nx, tab, cov, estimate, own_rows):
    blocks, stacked, width = estimate.shape
    count = blocks * (stacked // width)
    f32, bf16 = jnp.float32, jnp.bfloat16
    vmem = pl.BlockSpec(memory_space=pltpu.VMEM)
    smem = pl.BlockSpec(memory_space=pltpu.SMEM)
    return pl.pallas_call(
        functools.partial(steps_kernel, nx),
        out_shape=jax.ShapeDtypeStruct((blocks // nx, own_rows, width), f32),
        in_specs=[smem, vmem, vmem],
        out_specs=vmem,
        scratch_shapes=[
            pltpu.VMEM((PAIRS, width, width), bf16),
            pltpu.VMEM((PAIRS, width, width), bf16),
            pltpu.VMEM((count, width, width), f32),
            pltpu.VMEM((count, width, width), bf16),
            pltpu.VMEM((count, width, width), bf16),
            pltpu.VMEM((count, width, width), f32),
        ],
        compiler_params=pltpu.CompilerParams(vmem_limit_bytes=VMEM_STEPS),
    )(tab, cov, estimate)


def pair_tables(block_rows, counts):
    blocks, slots = block_rows.shape
    ids = jnp.arange(blocks, dtype=jnp.int32)
    live = jnp.arange(slots, dtype=jnp.int32)[None, :] < counts[:, None]
    has = jnp.any(live[:, :, None] & (block_rows[:, :, None] == ids), axis=1)
    need = jnp.any(has[:, :, None] & has[:, None, :], axis=0) & (ids[:, None] <= ids[None, :])
    flat = need.reshape(-1).astype(jnp.int32)
    order = jnp.arange(blocks * blocks, dtype=jnp.int32)
    rank = jnp.sum(jnp.where(order[None, :] < order[:, None], flat[None, :], 0), axis=1)
    hit = (flat[None, :] > 0) & (rank[None, :] == jnp.arange(PAIRS, dtype=jnp.int32)[:, None])
    which = jnp.sum(jnp.where(hit, order[None, :], 0), axis=1)
    return which // blocks, which % blocks, rank


def body(dims, samples, estimate, block_rows, counts, holder):
    nx, ny, nz = dims
    rows_dev, own_blocks, width = samples.shape
    samp_count = 2 * ny * nz
    blocks = holder.shape[0]
    slots = block_rows.shape[1]
    left, right, rank = pair_tables(block_rows, counts)
    ids = jnp.arange(blocks, dtype=jnp.int32)
    position = jnp.sum(jnp.where(holder[:, None] == ids[None, :], ids[:, None], 0), axis=0)
    own_rows = slots * width // samp_count
    first = lax.axis_index("samp") * own_rows
    place = jnp.stack([lax.axis_index("var"), first // width, first % width]).astype(jnp.int32)
    tab = jnp.concatenate([block_rows.reshape(-1), counts, holder, position, rank, left, right, place])
    own = samples.transpose(1, 0, 2)
    cov, every = exchange(dims, rows_dev * samp_count, tab, own, estimate)
    return steps(nx, tab, cov, every, own_rows)


def solution(mesh):
    nx = mesh.shape["var"]
    ny, nz = (8, 12) if mesh.shape["samp"] == 192 else (2, 2)
    return jax.shard_map(
        functools.partial(body, (nx, ny, nz)),
        mesh=mesh,
        in_specs=(P("samp", "var", None), P("var", None, None), P(), P(), P()),
        out_specs=P("var", "samp", None),
        check_vma=False,
    )
```

```python
import functools

import jax
import jax.numpy as jnp
from jax import lax
from jax.experimental import pallas as pl
from jax.experimental.pallas import tpu as pltpu
from jax.sharding import PartitionSpec as P

MESH = pl.DeviceIdType.MESH
ITERS = 2
PAIRS = 24
VMEM_EXCHANGE = 12 << 20
VMEM_STEPS = 34 << 20

TABLE, COUNTS, HOLDER, POSITION, RANK, LEFT, RIGHT, PLACE = 0, 24, 32, 40, 48, 112, 136, 160
step_size = 0.1
penalty = 5.0


def exchange_kernel(
    dims, sample_total, tab, own_ref, est_ref, cov_ref, all_ref,
    data, part, twin, acc, got1, mid, got2, share,
    x_send, x_recv, d_send, d_recv, s1_send, s1_recv, s2_send, s2_recv,
    e_send, e_recv, b_send, b_recv, r_send, r_recv, l_send, l_recv,
    t_send, t_recv, p_send, p_recv, pd_send, pd_recv, loc_sem,
):
    nx, ny, nz = dims
    s = lax.axis_index("samp")
    x = lax.axis_index("var")
    c = lax.rem(s, 2)
    z = lax.rem(s // 2, nz)
    y = s // (2 * nz)
    own_blocks = own_ref.shape[0]
    per_x = PAIRS // nx
    rows = acc.shape[0]
    half = rows // per_x

    def at(xx, yy, zz, cc):
        return ((yy * nz + zz) * 2 + cc, xx)

    def x_peer(k):
        return at(lax.rem(x + k, nx), y, z, c)

    def y_peer(k):
        return at(x, lax.rem(y + k, ny), z, c)

    def z_peer(k):
        return at(x, y, lax.rem(z + k, nz), c)

    sibling = at(x, y, z, 1 - c)

    def copy(src, dst, send, recv, device):
        return pltpu.make_async_remote_copy(
            src_ref=src, dst_ref=dst, send_sem=send, recv_sem=recv, device_id=device, device_id_type=MESH
        )

    barrier = pltpu.get_barrier_semaphore()
    for peer, n in ((x_peer, nx), (y_peer, ny), (z_peer, nz)):
        @pl.loop(1, n)
        def _(k, peer=peer):
            pl.semaphore_signal(barrier, inc=1, device_id=peer(k), device_id_type=MESH)
    pl.semaphore_signal(barrier, inc=1, device_id=sibling, device_id_type=MESH)
    pl.semaphore_wait(barrier, nx + ny + nz - 2)

    class Ring:
        def __init__(self, own_piece, piece, send, recv):
            right, left = lax.rem(x + 1, nx), lax.rem(x + nx - 1, nx)

            def to(k, owner, n, sem):
                src = own_piece(n) if owner is None else piece(owner, n)
                dst = piece(x if owner is None else owner, n)
                return copy(src, dst, send.at[sem], recv.at[sem], x_peer(k))

            self.own = [to(1, None, 0, 0), to(nx - 1, None, 1, 1), to(1, None, 1, 2), to(nx - 1, None, 0, 3)]
            self.onward = [to(1, left, 0, 4), to(nx - 1, right, 1, 5)]

        def start(self):
            for cp in self.own:
                cp.start()

        def forward(self):
            for n in range(2):
                self.own[n].wait_recv()
                self.onward[n].start()

        def finish(self):
            self.own[2].wait_recv()
            self.own[3].wait_recv()
            for cp in self.onward:
                cp.wait_recv()
            for cp in self.own + self.onward:
                cp.wait_send()

    mine = pl.ds(x * own_blocks, own_blocks)
    samples_ring = Ring(
        lambda n: own_ref.at[n], lambda owner, n: data.at[owner * own_blocks + n], x_send, x_recv
    )
    samples_ring.start()
    est_local = pltpu.make_async_copy(est_ref, all_ref.at[mine], loc_sem.at[0])
    est_local.start()
    data[mine] = own_ref[...]
    samples_ring.forward()
    samples_ring.finish()

    est_half = est_ref.shape[1] // 2

    def est_rows(n):
        return pl.ds(n * est_half, est_half)

    est_ring = Ring(
        lambda n: est_ref.at[c, est_rows(n)],
        lambda owner, n: all_ref.at[owner * own_blocks + c, est_rows(n)],
        p_send, p_recv,
    )
    est_ring.start()

    pair_copies = []
    for u in range(per_x):
        left = data[tab[LEFT + x * per_x + u]]
        right = data[tab[RIGHT + x * per_x + u]]
        prod = lax.dot_general(left, right, (((0,), (0,)), ((), ())), preferred_element_type=jnp.float32)
        part[0, u] = prod[:half]
        part[1, u] = prod[half:]
        cp = copy(part.at[1 - c, u], twin.at[u], d_send.at[u], d_recv.at[u], sibling)
        cp.start()
        pair_copies.append(cp)
    for u in range(per_x):
        pair_copies[u].wait()
        acc[u * half:(u + 1) * half] = part[c, u] + twin[u]

    def est_twin(k):
        ref = all_ref.at[lax.rem(x + k, nx) * own_blocks + c]
        return copy(ref, ref, pd_send.at[k - 1], pd_recv.at[k - 1], sibling)

    lane = own_ref.shape[2] // 2

    def lanes(g):
        return pl.ds(g * lane, lane)

    def reduce_and_gather(me_a, peer_a, n_a, me_b, peer_b, n_b, other_rows, other_n):
        rows_a = rows // n_a
        rows_b = rows_a // n_b
        groups = range(2)

        def each(n, action):
            @pl.loop(1, n)
            def _(k):
                action(k)

        def first(k, g):
            return copy(
                acc.at[pl.ds(lax.rem(me_a + k, n_a) * rows_a, rows_a), lanes(g)],
                got1.at[k - 1, pl.ds(0, rows_a), lanes(g)],
                s1_send.at[g, k - 1], s1_recv.at[g, k - 1], peer_a(k),
            )

        def second(k, g):
            return copy(
                mid.at[pl.ds(lax.rem(me_b + k, n_b) * rows_b, rows_b), lanes(g)], got2.at[k - 1, :, lanes(g)],
                s2_send.at[g, k - 1], s2_recv.at[g, k - 1], peer_b(k),
            )

        first_row = pl.multiple_of(me_a * rows_a + me_b * rows_b, 8)
        place = pl.ds(first_row, rows_b)

        def third(k, g):
            return copy(
                share.at[:, lanes(g)], cov_ref.at[x, c, place, lanes(g)],
                e_send.at[g, k - 1], e_recv.at[g, k - 1], x_peer(k),
            )

        def fourth(k, g):
            ref = cov_ref.at[:, c, place, lanes(g)]
            return copy(ref, ref, b_send.at[g, k - 1], b_recv.at[g, k - 1], peer_b(k))

        for g in groups:
            each(n_a, lambda k: first(k, g).start())
        for g in groups:
            here = slice(g * lane, (g + 1) * lane)
            mid[pl.ds(0, rows_a), here] = acc[pl.ds(pl.multiple_of(me_a * rows_a, 8), rows_a), here]

            def add_first(k):
                first(k, g).wait()
                mid[pl.ds(0, rows_a), here] += got1[k - 1, pl.ds(0, rows_a), here]

            each(n_a, add_first)
            each(n_b, lambda k: second(k, g).start())
        est_ring.forward()
        for g in groups:
            here = slice(g * lane, (g + 1) * lane)
            share[:, here] = mid[pl.ds(pl.multiple_of(me_b * rows_b, 8), rows_b), here]

            def add_second(k):
                second(k, g).wait()
                share[:, here] += got2[k - 1, :, here]

            each(n_b, add_second)
            share[:, here] = share[:, here] * (1.0 / sample_total)
            each(nx, lambda k: third(k, g).start())
            own_share = pltpu.make_async_copy(
                share.at[:, lanes(g)], cov_ref.at[x, c, place, lanes(g)], loc_sem.at[1 + g]
            )
            own_share.start()
            own_share.wait()
        for g in groups:
            each(nx, lambda k: third(k, g).wait())
            each(n_b, lambda k: fourth(k, g).start())

        def chunk(owner, h):
            return cov_ref.at[:, c, pl.ds(pl.multiple_of(owner * rows_a, 8), rows_a), lanes(h)]

        def ahead(t):
            return lax.rem(me_a + t, n_a)

        def behind(t):
            return lax.rem(me_a - t + n_a, n_a)

        def to_right(t, h):
            ref = chunk(behind(t), h)
            return copy(ref, ref, r_send.at[2 * t + h], r_recv.at[2 * t + h], peer_a(1))

        def to_left(t, h):
            ref = chunk(ahead(t), h)
            return copy(ref, ref, l_send.at[2 * t + h], l_recv.at[2 * t + h], peer_a(n_a - 1))

        def to_twin(owner, h):
            ref = chunk(owner, h)
            return copy(ref, ref, t_send.at[2 * owner + h], t_recv.at[2 * owner + h], sibling)

        whole = (n_a - 1) // 2
        right_steps = [(t, h) for t in range(whole) for h in range(2)]
        left_steps = list(right_steps)
        if n_a % 2 == 0:
            right_steps.append((whole, 0))
            left_steps.append((whole, 1))
        for t in range(whole + 1):
            for h in range(2):
                if t == 0:
                    each(n_b, lambda k: fourth(k, h).wait())
                if (t, h) in right_steps:
                    if t > 0:
                        to_right(t - 1, h).wait_recv()
                    to_right(t, h).start()
                    if t > 0:
                        to_twin(behind(t), h).start()
                if (t, h) in left_steps:
                    if t > 0:
                        to_left(t - 1, h).wait_recv()
                    to_left(t, h).start()
                    if t > 0:
                        to_twin(ahead(t), h).start()
                if t == 0:
                    to_twin(me_a, h).start()
            if t == 0:
                est_ring.finish()
                for k in range(1, nx):
                    est_twin(k).start()
        for t, h in right_steps:
            if (t + 1, h) not in right_steps:
                to_right(t, h).wait_recv()
                to_twin(behind(t + 1), h).start()
        for t, h in left_steps:
            if (t + 1, h) not in left_steps:
                to_left(t, h).wait_recv()
                to_twin(ahead(t + 1), h).start()
        for t, h in right_steps:
            to_right(t, h).wait_send()
        for t, h in left_steps:
            to_left(t, h).wait_send()

        @pl.loop(0, 2 * other_n)
        def _(n):
            ref = cov_ref.at[
                :, 1 - c, pl.ds(pl.multiple_of(n // 2 * other_rows, 8), other_rows),
                pl.ds(pl.multiple_of(lax.rem(n, 2) * lane, lane), lane),
            ]
            copy(ref, ref, t_send.at[n], t_recv.at[n], sibling).wait_recv()

        @pl.loop(0, 2 * n_a)
        def _(n):
            ref = cov_ref.at[
                :, c, pl.ds(pl.multiple_of(n // 2 * rows_a, 8), rows_a),
                pl.ds(pl.multiple_of(lax.rem(n, 2) * lane, lane), lane),
            ]
            copy(ref, ref, t_send.at[n], t_recv.at[n], sibling).wait_send()

    @pl.when(c == 0)
    def _():
        reduce_and_gather(y, y_peer, ny, z, z_peer, nz, rows // nz, nz)

    @pl.when(c == 1)
    def _():
        reduce_and_gather(z, z_peer, nz, y, y_peer, ny, rows // ny, ny)

    est_local.wait()
    for k in range(1, nx):
        est_twin(k).wait()


def exchange(dims, sample_total, tab, own, estimate):
    nx, ny, nz = dims
    own_blocks, rows_dev, width = own.shape
    blocks = own_blocks * nx
    per_x = PAIRS // nx
    half = width // 2
    rows = per_x * half
    most = max(ny, nz)
    dma = pltpu.SemaphoreType.DMA
    f32 = jnp.float32
    smem = pl.BlockSpec(memory_space=pltpu.SMEM)
    vmem = pl.BlockSpec(memory_space=pltpu.VMEM)
    hbm = pl.BlockSpec(memory_space=pl.ANY)
    return pl.pallas_call(
        functools.partial(exchange_kernel, dims, sample_total),
        out_shape=(
            jax.ShapeDtypeStruct((nx, 2, rows, width), f32),
            jax.ShapeDtypeStruct((blocks,) + estimate.shape[1:], f32),
        ),
        in_specs=[smem, vmem, hbm],
        out_specs=(hbm, hbm),
        scratch_shapes=[
            pltpu.VMEM((blocks, rows_dev, width), jnp.bfloat16),
            pltpu.VMEM((2, per_x, half, width), f32),
            pltpu.VMEM((per_x, half, width), f32),
            pltpu.VMEM((rows, width), f32),
            pltpu.VMEM((most - 1, rows // min(ny, nz), width), f32),
            pltpu.VMEM((rows // min(ny, nz), width), f32),
            pltpu.VMEM((most - 1, rows // (ny * nz), width), f32),
            pltpu.VMEM((rows // (ny * nz), width), f32),
            dma((6,)), dma((6,)),
            dma((per_x,)), dma((per_x,)),
            dma((2, most - 1)), dma((2, most - 1)),
            dma((2, most - 1)), dma((2, most - 1)),
            dma((2, nx - 1)), dma((2, nx - 1)),
            dma((2, most - 1)), dma((2, most - 1)),
            dma((2 * most,)), dma((2 * most,)),
            dma((2 * most,)), dma((2 * most,)),
            dma((2 * most,)), dma((2 * most,)),
            dma((6,)), dma((6,)),
            dma((nx - 1,)), dma((nx - 1,)),
            dma((3,)),
        ],
        compiler_params=pltpu.CompilerParams(
            collective_id=0, has_side_effects=True, vmem_limit_bytes=VMEM_EXCHANGE
        ),
    )(tab, own, estimate)


def steps_kernel(
    nx, tab, cov_ref, est_ref, out_ref,
    high, low, prec, weights, terms,
):
    blocks, stacked, width = est_ref.shape
    slots = stacked // width
    half = width // 2
    per_x = PAIRS // nx
    f32, bf16 = jnp.float32, jnp.bfloat16

    def row_of(j, s):
        return tab[TABLE + j * slots + s]

    def count(j):
        return tab[COUNTS + j]

    def holder(q):
        return tab[HOLDER + q]

    def position(i):
        return tab[POSITION + i]

    def pair_of(a, b):
        listed = tab[RANK + jnp.minimum(a, b) * blocks + jnp.maximum(a, b)]
        return listed + jnp.where(a <= b, 0, PAIRS)

    @pl.loop(0, PAIRS)
    def _(t):
        u = lax.rem(t, per_x)
        for h in range(2):
            value = cov_ref[t // per_x, h, pl.ds(pl.multiple_of(u * half, 8), half)]
            top = value.astype(bf16)
            high[t, h * half:(h + 1) * half] = top
            low[t, h * half:(h + 1) * half] = (value - top.astype(f32)).astype(bf16)

        @pl.when(tab[LEFT + t] != tab[RIGHT + t])
        def _():
            high[PAIRS + t] = high[t].T
            low[PAIRS + t] = low[t].T

    def block_of(q, s):
        return est_ref[q, pl.ds(pl.multiple_of(s * width, 8), width)]

    def mirror(j, i):
        return jnp.where(row_of(i, 0) == j, 0, jnp.where(row_of(i, 1) == j, 1, 2))

    def products(q, row_blocks, n, dests):
        j = holder(q)
        for i, dest in zip(row_blocks, dests):
            total = None
            for t in range(n):
                pair = pair_of(i, row_of(j, t))
                w = weights[q * slots + t]
                both = jnp.dot(high[pair], w, preferred_element_type=f32) + jnp.dot(
                    low[pair], w, preferred_element_type=f32
                )
                total = both if total is None else total + both
            terms[dest] = total

    def update(q, s, current):
        j = holder(q)
        i = row_of(j, s)
        other = position(i) * slots + mirror(j, i)
        gram = terms[q * slots + s] + terms[other].T
        stepped = current - (0.5 * step_size) * gram
        bound = step_size * penalty
        shrunk = jnp.maximum(stepped - bound, 0.0) + jnp.minimum(stepped + bound, 0.0)
        barrier = 0.5 * (stepped + jnp.sqrt(stepped * stepped + 4.0 * step_size))
        same = lax.broadcasted_iota(jnp.int32, (width, width), 0) == lax.broadcasted_iota(
            jnp.int32, (width, width), 1
        )
        return jnp.where(same & (i == j), barrier, shrunk)

    def live_blocks(action):
        @pl.loop(0, blocks * slots)
        def _(flat):
            q, s = flat // slots, lax.rem(flat, slots)

            @pl.when(s < count(holder(q)))
            def _():
                action(flat, q, s)

    def first_weights(flat, q, s):
        weights[flat] = block_of(q, s).astype(bf16)

    live_blocks(first_weights)

    for iteration in range(ITERS - 1):
        @pl.loop(0, blocks)
        def _(q):
            j = holder(q)
            for n in range(1, slots + 1):
                @pl.when(count(j) == n)
                def _():
                    products(q, [row_of(j, s) for s in range(n)], n, [q * slots + s for s in range(n)])

        def renew(flat, q, s):
            value = update(q, s, block_of(q, s) if iteration == 0 else prec[flat])
            prec[flat] = value
            weights[flat] = value.astype(bf16)

        live_blocks(renew)

    own_count, own_rows = out_ref.shape[0], out_ref.shape[1]
    s = tab[PLACE + 1]
    first_row = tab[PLACE + 2]

    def one_block(q, i, dest):
        for n in range(1, slots + 1):
            @pl.when(count(holder(q)) == n)
            def _():
                products(q, [i], n, [dest])

    for n in range(own_count):
        q = tab[PLACE] * own_count + n
        j = holder(q)
        live = s < count(j)

        @pl.when(live)
        def _():
            i = row_of(j, s)
            qi = position(i)
            one_block(q, i, q * slots + s)

            @pl.when(i != j)
            def _():
                one_block(qi, j, qi * slots + mirror(j, i))

            terms[q * slots + s] = update(q, s, prec[q * slots + s])
            if own_rows % 8 == 0:
                out_ref[n] = terms[q * slots + s, pl.ds(pl.multiple_of(first_row, 8), own_rows)]
            else:
                eight = terms[q * slots + s, pl.ds(pl.multiple_of(first_row // 8 * 8, 8), 8)]
                out_ref[n] = jnp.where(lax.rem(first_row, 8) == 0, eight[:own_rows], eight[8 - own_rows:])

        @pl.when(jnp.logical_not(live))
        def _():
            out_ref[n] = jnp.zeros(out_ref.shape[1:], f32)


def steps(nx, tab, cov, estimate, own_rows):
    blocks, stacked, width = estimate.shape
    count = blocks * (stacked // width)
    f32, bf16 = jnp.float32, jnp.bfloat16
    vmem = pl.BlockSpec(memory_space=pltpu.VMEM)
    smem = pl.BlockSpec(memory_space=pltpu.SMEM)
    return pl.pallas_call(
        functools.partial(steps_kernel, nx),
        out_shape=jax.ShapeDtypeStruct((blocks // nx, own_rows, width), f32),
        in_specs=[smem, vmem, vmem],
        out_specs=vmem,
        scratch_shapes=[
            pltpu.VMEM((2 * PAIRS, width, width), bf16),
            pltpu.VMEM((2 * PAIRS, width, width), bf16),
            pltpu.VMEM((count, width, width), f32),
            pltpu.VMEM((count, width, width), bf16),
            pltpu.VMEM((count, width, width), f32),
        ],
        compiler_params=pltpu.CompilerParams(vmem_limit_bytes=VMEM_STEPS),
    )(tab, cov, estimate)


def pair_tables(block_rows, counts):
    blocks, slots = block_rows.shape
    ids = jnp.arange(blocks, dtype=jnp.int32)
    live = jnp.arange(slots, dtype=jnp.int32)[None, :] < counts[:, None]
    has = jnp.any(live[:, :, None] & (block_rows[:, :, None] == ids), axis=1)
    need = jnp.any(has[:, :, None] & has[:, None, :], axis=0) & (ids[:, None] <= ids[None, :])
    flat = need.reshape(-1).astype(jnp.int32)
    order = jnp.arange(blocks * blocks, dtype=jnp.int32)
    rank = jnp.sum(jnp.where(order[None, :] < order[:, None], flat[None, :], 0), axis=1)
    hit = (flat[None, :] > 0) & (rank[None, :] == jnp.arange(PAIRS, dtype=jnp.int32)[:, None])
    which = jnp.sum(jnp.where(hit, order[None, :], 0), axis=1)
    return which // blocks, which % blocks, rank


def body(dims, samples, estimate, block_rows, counts, holder):
    nx, ny, nz = dims
    rows_dev, own_blocks, width = samples.shape
    samp_count = 2 * ny * nz
    blocks = holder.shape[0]
    slots = block_rows.shape[1]
    left, right, rank = pair_tables(block_rows, counts)
    ids = jnp.arange(blocks, dtype=jnp.int32)
    position = jnp.sum(jnp.where(holder[:, None] == ids[None, :], ids[:, None], 0), axis=0)
    own_rows = slots * width // samp_count
    first = lax.axis_index("samp") * own_rows
    place = jnp.stack([lax.axis_index("var"), first // width, first % width]).astype(jnp.int32)
    tab = jnp.concatenate([block_rows.reshape(-1), counts, holder, position, rank, left, right, place])
    own = samples.transpose(1, 0, 2)
    cov, every = exchange(dims, rows_dev * samp_count, tab, own, estimate)
    return steps(nx, tab, cov, every, own_rows)


def solution(mesh):
    nx = mesh.shape["var"]
    ny, nz = (8, 12) if mesh.shape["samp"] == 192 else (2, 2)
    return jax.shard_map(
        functools.partial(body, (nx, ny, nz)),
        mesh=mesh,
        in_specs=(P("samp", "var", None), P("var", None, None), P(), P(), P()),
        out_specs=P("var", "samp", None),
        check_vma=False,
    )
```

```python
import functools

import jax
import jax.numpy as jnp
from jax import lax
from jax.experimental import pallas as pl
from jax.experimental.pallas import tpu as pltpu
from jax.sharding import PartitionSpec as P

MESH = pl.DeviceIdType.MESH
ITERS = 2
PAIRS = 24
VMEM_EXCHANGE = 12 << 20
VMEM_STEPS = 34 << 20

TABLE, COUNTS, HOLDER, POSITION, RANK, LEFT, RIGHT, PLACE = 0, 24, 32, 40, 48, 112, 136, 160
step_size = 0.1
penalty = 5.0


def exchange_kernel(
    dims, sample_total, tab, own_ref, est_ref, cov_ref, all_ref,
    data, part, twin, acc, got1, mid, got2, share,
    x_send, x_recv, d_send, d_recv, s1_send, s1_recv, s2_send, s2_recv,
    e_send, e_recv, b_send, b_recv, r_send, r_recv, l_send, l_recv,
    t_send, t_recv, p_send, p_recv, pd_send, pd_recv, loc_sem,
):
    nx, ny, nz = dims
    s = lax.axis_index("samp")
    x = lax.axis_index("var")
    c = lax.rem(s, 2)
    z = lax.rem(s // 2, nz)
    y = s // (2 * nz)
    own_blocks = own_ref.shape[0]
    per_x = PAIRS // nx
    rows = acc.shape[0]
    half = rows // per_x

    def at(xx, yy, zz, cc):
        return ((yy * nz + zz) * 2 + cc, xx)

    def x_peer(k):
        return at(lax.rem(x + k, nx), y, z, c)

    def y_peer(k):
        return at(x, lax.rem(y + k, ny), z, c)

    def z_peer(k):
        return at(x, y, lax.rem(z + k, nz), c)

    sibling = at(x, y, z, 1 - c)

    def copy(src, dst, send, recv, device):
        return pltpu.make_async_remote_copy(
            src_ref=src, dst_ref=dst, send_sem=send, recv_sem=recv, device_id=device, device_id_type=MESH
        )

    barrier = pltpu.get_barrier_semaphore()
    for peer, n in ((x_peer, nx), (y_peer, ny), (z_peer, nz)):
        @pl.loop(1, n)
        def _(k, peer=peer):
            pl.semaphore_signal(barrier, inc=1, device_id=peer(k), device_id_type=MESH)
    pl.semaphore_signal(barrier, inc=1, device_id=sibling, device_id_type=MESH)
    pl.semaphore_wait(barrier, nx + ny + nz - 2)

    class Ring:
        def __init__(self, own_piece, piece, send, recv):
            right, left = lax.rem(x + 1, nx), lax.rem(x + nx - 1, nx)

            def to(k, owner, n, sem):
                src = own_piece(n) if owner is None else piece(owner, n)
                dst = piece(x if owner is None else owner, n)
                return copy(src, dst, send.at[sem], recv.at[sem], x_peer(k))

            self.own = [to(1, None, 0, 0), to(nx - 1, None, 1, 1), to(1, None, 1, 2), to(nx - 1, None, 0, 3)]
            self.onward = [to(1, left, 0, 4), to(nx - 1, right, 1, 5)]

        def start(self):
            for cp in self.own:
                cp.start()

        def forward(self):
            for n in range(2):
                self.own[n].wait_recv()
                self.onward[n].start()

        def finish(self):
            self.own[2].wait_recv()
            self.own[3].wait_recv()
            for cp in self.onward:
                cp.wait_recv()
            for cp in self.own + self.onward:
                cp.wait_send()

    mine = pl.ds(x * own_blocks, own_blocks)
    samples_ring = Ring(
        lambda n: own_ref.at[n], lambda owner, n: data.at[owner * own_blocks + n], x_send, x_recv
    )
    samples_ring.start()
    est_local = pltpu.make_async_copy(est_ref, all_ref.at[mine], loc_sem.at[0])
    est_local.start()
    data[mine] = own_ref[...]
    samples_ring.forward()
    samples_ring.finish()

    est_half = est_ref.shape[1] // 2

    def est_rows(n):
        return pl.ds(n * est_half, est_half)

    est_ring = Ring(
        lambda n: est_ref.at[c, est_rows(n)],
        lambda owner, n: all_ref.at[owner * own_blocks + c, est_rows(n)],
        p_send, p_recv,
    )
    est_ring.start()

    pair_copies = []
    for u in range(per_x):
        left = data[tab[LEFT + x * per_x + u]]
        right = data[tab[RIGHT + x * per_x + u]]
        prod = lax.dot_general(left, right, (((0,), (0,)), ((), ())), preferred_element_type=jnp.float32)
        part[0, u] = prod[:half]
        part[1, u] = prod[half:]
        cp = copy(part.at[1 - c, u], twin.at[u], d_send.at[u], d_recv.at[u], sibling)
        cp.start()
        pair_copies.append(cp)
    for u in range(per_x):
        pair_copies[u].wait()
        acc[u * half:(u + 1) * half] = part[c, u] + twin[u]

    def est_twin(k):
        ref = all_ref.at[lax.rem(x + k, nx) * own_blocks + c]
        return copy(ref, ref, pd_send.at[k - 1], pd_recv.at[k - 1], sibling)

    lane = own_ref.shape[2] // 2

    def lanes(g):
        return pl.ds(g * lane, lane)

    def reduce_and_gather(me_a, peer_a, n_a, me_b, peer_b, n_b, other_rows, other_n):
        rows_a = rows // n_a
        rows_b = rows_a // n_b
        groups = range(2)

        def each(n, action):
            @pl.loop(1, n)
            def _(k):
                action(k)

        def first(k, g):
            return copy(
                acc.at[pl.ds(lax.rem(me_a + k, n_a) * rows_a, rows_a), lanes(g)],
                got1.at[k - 1, pl.ds(0, rows_a), lanes(g)],
                s1_send.at[g, k - 1], s1_recv.at[g, k - 1], peer_a(k),
            )

        def second(k, g):
            return copy(
                mid.at[pl.ds(lax.rem(me_b + k, n_b) * rows_b, rows_b), lanes(g)], got2.at[k - 1, :, lanes(g)],
                s2_send.at[g, k - 1], s2_recv.at[g, k - 1], peer_b(k),
            )

        first_row = pl.multiple_of(me_a * rows_a + me_b * rows_b, 8)
        place = pl.ds(first_row, rows_b)

        def third(k, g):
            return copy(
                share.at[:, lanes(g)], cov_ref.at[x, c, place, lanes(g)],
                e_send.at[g, k - 1], e_recv.at[g, k - 1], x_peer(k),
            )

        def fourth(k, g):
            ref = cov_ref.at[:, c, place, lanes(g)]
            return copy(ref, ref, b_send.at[g, k - 1], b_recv.at[g, k - 1], peer_b(k))

        for g in groups:
            each(n_a, lambda k: first(k, g).start())
        est_ring.forward()
        for g in groups:
            here = slice(g * lane, (g + 1) * lane)
            mid[pl.ds(0, rows_a), here] = acc[pl.ds(pl.multiple_of(me_a * rows_a, 8), rows_a), here]

            def add_first(k):
                first(k, g).wait()
                mid[pl.ds(0, rows_a), here] += got1[k - 1, pl.ds(0, rows_a), here]

            each(n_a, add_first)
            each(n_b, lambda k: second(k, g).start())
        for g in groups:
            here = slice(g * lane, (g + 1) * lane)
            share[:, here] = mid[pl.ds(pl.multiple_of(me_b * rows_b, 8), rows_b), here]

            def add_second(k):
                second(k, g).wait()
                share[:, here] += got2[k - 1, :, here]

            each(n_b, add_second)
            share[:, here] = share[:, here] * (1.0 / sample_total)
            each(nx, lambda k: third(k, g).start())
            own_share = pltpu.make_async_copy(
                share.at[:, lanes(g)], cov_ref.at[x, c, place, lanes(g)], loc_sem.at[1 + g]
            )
            own_share.start()
            own_share.wait()
        for g in groups:
            each(nx, lambda k: third(k, g).wait())
            each(n_b, lambda k: fourth(k, g).start())

        def chunk(owner, h):
            return cov_ref.at[:, c, pl.ds(pl.multiple_of(owner * rows_a, 8), rows_a), lanes(h)]

        def ahead(t):
            return lax.rem(me_a + t, n_a)

        def behind(t):
            return lax.rem(me_a - t + n_a, n_a)

        def to_right(t, h):
            ref = chunk(behind(t), h)
            return copy(ref, ref, r_send.at[2 * t + h], r_recv.at[2 * t + h], peer_a(1))

        def to_left(t, h):
            ref = chunk(ahead(t), h)
            return copy(ref, ref, l_send.at[2 * t + h], l_recv.at[2 * t + h], peer_a(n_a - 1))

        def to_twin(owner, h):
            ref = chunk(owner, h)
            return copy(ref, ref, t_send.at[2 * owner + h], t_recv.at[2 * owner + h], sibling)

        whole = (n_a - 1) // 2
        right_steps = [(t, h) for t in range(whole) for h in range(2)]
        left_steps = list(right_steps)
        if n_a % 2 == 0:
            right_steps.append((whole, 0))
            left_steps.append((whole, 1))
        for t in range(whole + 1):
            for h in range(2):
                if t == 0:
                    each(n_b, lambda k: fourth(k, h).wait())
                if (t, h) in right_steps:
                    if t > 0:
                        to_right(t - 1, h).wait_recv()
                    to_right(t, h).start()
                    if t > 0:
                        to_twin(behind(t), h).start()
                if (t, h) in left_steps:
                    if t > 0:
                        to_left(t - 1, h).wait_recv()
                    to_left(t, h).start()
                    if t > 0:
                        to_twin(ahead(t), h).start()
                if t == 0:
                    to_twin(me_a, h).start()
            if t == 0:
                est_ring.finish()
                for k in range(1, nx):
                    est_twin(k).start()
        for t, h in right_steps:
            if (t + 1, h) not in right_steps:
                to_right(t, h).wait_recv()
                to_twin(behind(t + 1), h).start()
        for t, h in left_steps:
            if (t + 1, h) not in left_steps:
                to_left(t, h).wait_recv()
                to_twin(ahead(t + 1), h).start()
        for t, h in right_steps:
            to_right(t, h).wait_send()
        for t, h in left_steps:
            to_left(t, h).wait_send()

        @pl.loop(0, 2 * other_n)
        def _(n):
            ref = cov_ref.at[
                :, 1 - c, pl.ds(pl.multiple_of(n // 2 * other_rows, 8), other_rows),
                pl.ds(pl.multiple_of(lax.rem(n, 2) * lane, lane), lane),
            ]
            copy(ref, ref, t_send.at[n], t_recv.at[n], sibling).wait_recv()

        @pl.loop(0, 2 * n_a)
        def _(n):
            ref = cov_ref.at[
                :, c, pl.ds(pl.multiple_of(n // 2 * rows_a, 8), rows_a),
                pl.ds(pl.multiple_of(lax.rem(n, 2) * lane, lane), lane),
            ]
            copy(ref, ref, t_send.at[n], t_recv.at[n], sibling).wait_send()

    @pl.when(c == 0)
    def _():
        reduce_and_gather(y, y_peer, ny, z, z_peer, nz, rows // nz, nz)

    @pl.when(c == 1)
    def _():
        reduce_and_gather(z, z_peer, nz, y, y_peer, ny, rows // ny, ny)

    est_local.wait()
    for k in range(1, nx):
        est_twin(k).wait()


def exchange(dims, sample_total, tab, own, estimate):
    nx, ny, nz = dims
    own_blocks, rows_dev, width = own.shape
    blocks = own_blocks * nx
    per_x = PAIRS // nx
    half = width // 2
    rows = per_x * half
    most = max(ny, nz)
    dma = pltpu.SemaphoreType.DMA
    f32 = jnp.float32
    smem = pl.BlockSpec(memory_space=pltpu.SMEM)
    vmem = pl.BlockSpec(memory_space=pltpu.VMEM)
    hbm = pl.BlockSpec(memory_space=pl.ANY)
    return pl.pallas_call(
        functools.partial(exchange_kernel, dims, sample_total),
        out_shape=(
            jax.ShapeDtypeStruct((nx, 2, rows, width), f32),
            jax.ShapeDtypeStruct((blocks,) + estimate.shape[1:], f32),
        ),
        in_specs=[smem, vmem, pl.BlockSpec(memory_space=pltpu.HBM)],
        out_specs=(hbm, hbm),
        scratch_shapes=[
            pltpu.VMEM((blocks, rows_dev, width), jnp.bfloat16),
            pltpu.VMEM((2, per_x, half, width), f32),
            pltpu.VMEM((per_x, half, width), f32),
            pltpu.VMEM((rows, width), f32),
            pltpu.VMEM((most - 1, rows // min(ny, nz), width), f32),
            pltpu.VMEM((rows // min(ny, nz), width), f32),
            pltpu.VMEM((most - 1, rows // (ny * nz), width), f32),
            pltpu.VMEM((rows // (ny * nz), width), f32),
            dma((6,)), dma((6,)),
            dma((per_x,)), dma((per_x,)),
            dma((2, most - 1)), dma((2, most - 1)),
            dma((2, most - 1)), dma((2, most - 1)),
            dma((2, nx - 1)), dma((2, nx - 1)),
            dma((2, most - 1)), dma((2, most - 1)),
            dma((2 * most,)), dma((2 * most,)),
            dma((2 * most,)), dma((2 * most,)),
            dma((2 * most,)), dma((2 * most,)),
            dma((6,)), dma((6,)),
            dma((nx - 1,)), dma((nx - 1,)),
            dma((3,)),
        ],
        compiler_params=pltpu.CompilerParams(
            collective_id=0, has_side_effects=True, vmem_limit_bytes=VMEM_EXCHANGE
        ),
    )(tab, own, estimate)


def steps_kernel(
    nx, tab, cov_ref, est_ref, out_ref,
    high, low, prec, weights, terms,
):
    blocks, stacked, width = est_ref.shape
    slots = stacked // width
    half = width // 2
    per_x = PAIRS // nx
    f32, bf16 = jnp.float32, jnp.bfloat16

    def row_of(j, s):
        return tab[TABLE + s * blocks + j]

    def count(j):
        return tab[COUNTS + j]

    def holder(q):
        return tab[HOLDER + q]

    def position(i):
        return tab[POSITION + i]

    def pair_of(a, b):
        listed = tab[RANK + jnp.minimum(a, b) * blocks + jnp.maximum(a, b)]
        return listed + jnp.where(a <= b, 0, PAIRS)

    @pl.loop(0, PAIRS)
    def _(t):
        u = lax.rem(t, per_x)
        for h in range(2):
            value = cov_ref[t // per_x, h, pl.ds(pl.multiple_of(u * half, 8), half)]
            top = value.astype(bf16)
            high[t, h * half:(h + 1) * half] = top
            low[t, h * half:(h + 1) * half] = (value - top.astype(f32)).astype(bf16)

        @pl.when(tab[LEFT + t] != tab[RIGHT + t])
        def _():
            high[PAIRS + t] = high[t].T
            low[PAIRS + t] = low[t].T

    def block_of(q, s):
        return est_ref[q, pl.ds(pl.multiple_of(s * width, 8), width)]

    def mirror(j, i):
        return jnp.where(row_of(i, 0) == j, 0, jnp.where(row_of(i, 1) == j, 1, 2))

    def products(q, row_blocks, n, dests):
        j = holder(q)
        for i, dest in zip(row_blocks, dests):
            total = None
            for t in range(n):
                pair = pair_of(i, row_of(j, t))
                w = weights[q * slots + t]
                both = jnp.dot(high[pair], w, preferred_element_type=f32) + jnp.dot(
                    low[pair], w, preferred_element_type=f32
                )
                total = both if total is None else total + both
            terms[dest] = total

    def update(q, s, current):
        j = holder(q)
        i = row_of(j, s)
        other = position(i) * slots + mirror(j, i)
        gram = terms[q * slots + s] + terms[other].T
        stepped = current - (0.5 * step_size) * gram
        bound = step_size * penalty
        shrunk = jnp.maximum(stepped - bound, 0.0) + jnp.minimum(stepped + bound, 0.0)
        barrier = 0.5 * (stepped + jnp.sqrt(stepped * stepped + 4.0 * step_size))
        same = lax.broadcasted_iota(jnp.int32, (width, width), 0) == lax.broadcasted_iota(
            jnp.int32, (width, width), 1
        )
        return jnp.where(same & (i == j), barrier, shrunk)

    def live_blocks(action):
        @pl.loop(0, blocks * slots)
        def _(flat):
            q, s = flat // slots, lax.rem(flat, slots)

            @pl.when(s < count(holder(q)))
            def _():
                action(flat, q, s)

    def first_weights(flat, q, s):
        weights[flat] = block_of(q, s).astype(bf16)

    live_blocks(first_weights)

    for iteration in range(ITERS - 1):
        @pl.loop(0, blocks)
        def _(q):
            j = holder(q)
            for n in range(1, slots + 1):
                @pl.when(count(j) == n)
                def _():
                    products(q, [row_of(j, s) for s in range(n)], n, [q * slots + s for s in range(n)])

        def renew(flat, q, s):
            value = update(q, s, block_of(q, s) if iteration == 0 else prec[flat])
            prec[flat] = value
            weights[flat] = value.astype(bf16)

        live_blocks(renew)

    own_count, own_rows = out_ref.shape[0], out_ref.shape[1]
    s = tab[PLACE + 1]
    first_row = tab[PLACE + 2]

    def one_block(q, i, dest):
        for n in range(1, slots + 1):
            @pl.when(count(holder(q)) == n)
            def _():
                products(q, [i], n, [dest])

    for n in range(own_count):
        q = tab[PLACE] * own_count + n
        j = holder(q)
        live = s < count(j)

        @pl.when(live)
        def _():
            i = row_of(j, s)
            qi = position(i)
            one_block(q, i, q * slots + s)

            @pl.when(i != j)
            def _():
                one_block(qi, j, qi * slots + mirror(j, i))

            terms[q * slots + s] = update(q, s, prec[q * slots + s])
            if own_rows % 8 == 0:
                out_ref[n] = terms[q * slots + s, pl.ds(pl.multiple_of(first_row, 8), own_rows)]
            else:
                eight = terms[q * slots + s, pl.ds(pl.multiple_of(first_row // 8 * 8, 8), 8)]
                out_ref[n] = jnp.where(lax.rem(first_row, 8) == 0, eight[:own_rows], eight[8 - own_rows:])

        @pl.when(jnp.logical_not(live))
        def _():
            out_ref[n] = jnp.zeros(out_ref.shape[1:], f32)


def steps(nx, tab, cov, estimate, own_rows):
    blocks, stacked, width = estimate.shape
    count = blocks * (stacked // width)
    f32, bf16 = jnp.float32, jnp.bfloat16
    vmem = pl.BlockSpec(memory_space=pltpu.VMEM)
    smem = pl.BlockSpec(memory_space=pltpu.SMEM)
    return pl.pallas_call(
        functools.partial(steps_kernel, nx),
        out_shape=jax.ShapeDtypeStruct((blocks // nx, own_rows, width), f32),
        in_specs=[smem, vmem, vmem],
        out_specs=vmem,
        scratch_shapes=[
            pltpu.VMEM((2 * PAIRS, width, width), bf16),
            pltpu.VMEM((2 * PAIRS, width, width), bf16),
            pltpu.VMEM((count, width, width), f32),
            pltpu.VMEM((count, width, width), bf16),
            pltpu.VMEM((count, width, width), f32),
        ],
        compiler_params=pltpu.CompilerParams(vmem_limit_bytes=VMEM_STEPS),
    )(tab, cov, estimate)


def pair_tables(block_rows, counts):
    blocks, slots = block_rows.shape
    ids = jnp.arange(blocks, dtype=jnp.int32)
    live = jnp.arange(slots, dtype=jnp.int32)[None, :] < counts[:, None]
    has = jnp.any(live[:, :, None] & (block_rows[:, :, None] == ids), axis=1)
    need = jnp.any(has[:, :, None] & has[:, None, :], axis=0) & (ids[:, None] <= ids[None, :])
    flat = need.reshape(-1).astype(jnp.int32)
    order = jnp.arange(blocks * blocks, dtype=jnp.int32)
    rank = jnp.sum(jnp.where(order[None, :] < order[:, None], flat[None, :], 0), axis=1)
    hit = (flat[None, :] > 0) & (rank[None, :] == jnp.arange(PAIRS, dtype=jnp.int32)[:, None])
    which = jnp.sum(jnp.where(hit, order[None, :], 0), axis=1)
    return which // blocks, which % blocks, rank


def integer_table(block_rows, counts, holder, own_rows, width):
    blocks, slots = block_rows.shape
    raw = jnp.concatenate([block_rows[:, s] for s in range(slots)] + [counts, holder])
    raw = lax.optimization_barrier(raw)
    columns = raw.reshape(slots + 2, blocks)
    left, right, rank = pair_tables(columns[:slots].T, columns[slots])
    ids = jnp.arange(blocks, dtype=jnp.int32)
    position = jnp.sum(jnp.where(columns[slots + 1][:, None] == ids[None, :], ids[:, None], 0), axis=0)
    first = lax.axis_index("samp") * own_rows
    place = jnp.stack([lax.axis_index("var"), first // width, first % width]).astype(jnp.int32)
    return jnp.concatenate([raw, position, rank, left, right, place])


def body(dims, samples, estimate, block_rows, counts, holder):
    nx, ny, nz = dims
    rows_dev, _, width = samples.shape
    samp_count = 2 * ny * nz
    own_rows = block_rows.shape[1] * width // samp_count
    tab = integer_table(block_rows, counts, holder, own_rows, width)
    own = samples.transpose(1, 0, 2)
    cov, every = exchange(dims, rows_dev * samp_count, tab, own, estimate)
    return steps(nx, tab, cov, every, own_rows)


def solution(mesh):
    nx = mesh.shape["var"]
    ny, nz = (8, 12) if mesh.shape["samp"] == 192 else (2, 2)
    return jax.shard_map(
        functools.partial(body, (nx, ny, nz)),
        mesh=mesh,
        in_specs=(P("samp", "var", None), P("var", None, None), P(), P(), P()),
        out_specs=P("var", "samp", None),
        check_vma=False,
    )
```

```python
import functools

import jax
import jax.numpy as jnp
from jax import lax
from jax.experimental import pallas as pl
from jax.experimental.pallas import tpu as pltpu
from jax.sharding import PartitionSpec as P

MESH = pl.DeviceIdType.MESH
ITERS = 2
PAIRS = 24
VMEM_EXCHANGE = 12 << 20
VMEM_STEPS = 34 << 20

TABLE, COUNTS, HOLDER, POSITION, RANK, LEFT, RIGHT, PLACE = 0, 24, 32, 40, 48, 112, 136, 160
step_size = 0.1
penalty = 5.0


def exchange_kernel(
    dims, sample_total, tab, own_ref, est_ref, cov_ref, all_ref,
    data, part, twin, acc, got1, mid, got2, share,
    x_send, x_recv, d_send, d_recv, s1_send, s1_recv, s2_send, s2_recv,
    e_send, e_recv, b_send, b_recv, r_send, r_recv, l_send, l_recv,
    t_send, t_recv, p_send, p_recv, pd_send, pd_recv, loc_sem,
):
    nx, ny, nz = dims
    s = lax.axis_index("samp")
    x = lax.axis_index("var")
    c = lax.rem(s, 2)
    z = lax.rem(s // 2, nz)
    y = s // (2 * nz)
    own_blocks = own_ref.shape[0]
    per_x = PAIRS // nx
    rows = acc.shape[0]
    half = rows // per_x

    def at(xx, yy, zz, cc):
        return ((yy * nz + zz) * 2 + cc, xx)

    def x_peer(k):
        return at(lax.rem(x + k, nx), y, z, c)

    def y_peer(k):
        return at(x, lax.rem(y + k, ny), z, c)

    def z_peer(k):
        return at(x, y, lax.rem(z + k, nz), c)

    sibling = at(x, y, z, 1 - c)

    def copy(src, dst, send, recv, device):
        return pltpu.make_async_remote_copy(
            src_ref=src, dst_ref=dst, send_sem=send, recv_sem=recv, device_id=device, device_id_type=MESH
        )

    barrier = pltpu.get_barrier_semaphore()
    for peer, n in ((x_peer, nx), (y_peer, ny), (z_peer, nz)):
        @pl.loop(1, n)
        def _(k, peer=peer):
            pl.semaphore_signal(barrier, inc=1, device_id=peer(k), device_id_type=MESH)
    pl.semaphore_signal(barrier, inc=1, device_id=sibling, device_id_type=MESH)
    pl.semaphore_wait(barrier, nx + ny + nz - 2)

    class Ring:
        def __init__(self, own_piece, piece, send, recv):
            right, left = lax.rem(x + 1, nx), lax.rem(x + nx - 1, nx)

            def to(k, owner, n, sem):
                src = own_piece(n) if owner is None else piece(owner, n)
                dst = piece(x if owner is None else owner, n)
                return copy(src, dst, send.at[sem], recv.at[sem], x_peer(k))

            self.own = [to(1, None, 0, 0), to(nx - 1, None, 1, 1), to(1, None, 1, 2), to(nx - 1, None, 0, 3)]
            self.onward = [to(1, left, 0, 4), to(nx - 1, right, 1, 5)]

        def start(self):
            for cp in self.own:
                cp.start()

        def forward(self):
            for n in range(2):
                self.own[n].wait_recv()
                self.onward[n].start()

        def finish(self):
            self.own[2].wait_recv()
            self.own[3].wait_recv()
            for cp in self.onward:
                cp.wait_recv()
            for cp in self.own + self.onward:
                cp.wait_send()

    mine = pl.ds(x * own_blocks, own_blocks)
    samples_ring = Ring(
        lambda n: own_ref.at[n], lambda owner, n: data.at[owner * own_blocks + n], x_send, x_recv
    )
    samples_ring.start()
    est_local = pltpu.make_async_copy(est_ref, all_ref.at[mine], loc_sem.at[0])
    est_local.start()
    data[mine] = own_ref[...]
    samples_ring.forward()
    samples_ring.finish()

    est_half = est_ref.shape[1] // 2

    def est_rows(n):
        return pl.ds(n * est_half, est_half)

    est_ring = Ring(
        lambda n: est_ref.at[c, est_rows(n)],
        lambda owner, n: all_ref.at[owner * own_blocks + c, est_rows(n)],
        p_send, p_recv,
    )
    est_ring.start()

    pair_copies = []
    for u in range(per_x):
        left = data[tab[LEFT + x * per_x + u]]
        right = data[tab[RIGHT + x * per_x + u]]
        prod = lax.dot_general(left, right, (((0,), (0,)), ((), ())), preferred_element_type=jnp.float32)
        part[0, u] = prod[:half]
        part[1, u] = prod[half:]
        cp = copy(part.at[1 - c, u], twin.at[u], d_send.at[u], d_recv.at[u], sibling)
        cp.start()
        pair_copies.append(cp)
    for u in range(per_x):
        pair_copies[u].wait()
        acc[u * half:(u + 1) * half] = part[c, u] + twin[u]

    def est_twin(k):
        ref = all_ref.at[lax.rem(x + k, nx) * own_blocks + c]
        return copy(ref, ref, pd_send.at[k - 1], pd_recv.at[k - 1], sibling)

    lane = own_ref.shape[2] // 2

    def lanes(g):
        return pl.ds(g * lane, lane)

    def reduce_and_gather(me_a, peer_a, n_a, me_b, peer_b, n_b, other_rows, other_n):
        rows_a = rows // n_a
        rows_b = rows_a // n_b
        groups = range(2)

        def each(n, action):
            @pl.loop(1, n)
            def _(k):
                action(k)

        def first(k, g):
            return copy(
                acc.at[pl.ds(lax.rem(me_a + k, n_a) * rows_a, rows_a), lanes(g)],
                got1.at[k - 1, pl.ds(0, rows_a), lanes(g)],
                s1_send.at[g, k - 1], s1_recv.at[g, k - 1], peer_a(k),
            )

        def second(k, g):
            return copy(
                mid.at[pl.ds(lax.rem(me_b + k, n_b) * rows_b, rows_b), lanes(g)], got2.at[k - 1, :, lanes(g)],
                s2_send.at[g, k - 1], s2_recv.at[g, k - 1], peer_b(k),
            )

        first_row = pl.multiple_of(me_a * rows_a + me_b * rows_b, 8)
        place = pl.ds(first_row, rows_b)

        def third(k, g):
            return copy(
                share.at[:, lanes(g)], cov_ref.at[x, c, place, lanes(g)],
                e_send.at[g, k - 1], e_recv.at[g, k - 1], x_peer(k),
            )

        def fourth(k, g):
            ref = cov_ref.at[:, c, place, lanes(g)]
            return copy(ref, ref, b_send.at[g, k - 1], b_recv.at[g, k - 1], peer_b(k))

        for g in groups:
            each(n_a, lambda k: first(k, g).start())
        est_ring.forward()
        for g in groups:
            here = slice(g * lane, (g + 1) * lane)
            mid[pl.ds(0, rows_a), here] = acc[pl.ds(pl.multiple_of(me_a * rows_a, 8), rows_a), here]

            def add_first(k):
                first(k, g).wait()
                mid[pl.ds(0, rows_a), here] += got1[k - 1, pl.ds(0, rows_a), here]

            each(n_a, add_first)
            each(n_b, lambda k: second(k, g).start())
        for g in groups:
            here = slice(g * lane, (g + 1) * lane)
            share[:, here] = mid[pl.ds(pl.multiple_of(me_b * rows_b, 8), rows_b), here]

            def add_second(k):
                second(k, g).wait()
                share[:, here] += got2[k - 1, :, here]

            each(n_b, add_second)
            share[:, here] = share[:, here] * (1.0 / sample_total)
            each(nx, lambda k: third(k, g).start())
            own_share = pltpu.make_async_copy(
                share.at[:, lanes(g)], cov_ref.at[x, c, place, lanes(g)], loc_sem.at[1 + g]
            )
            own_share.start()
            own_share.wait()
        for g in groups:
            each(nx, lambda k: third(k, g).wait())
            each(n_b, lambda k: fourth(k, g).start())

        def chunk(owner, h):
            return cov_ref.at[:, c, pl.ds(pl.multiple_of(owner * rows_a, 8), rows_a), lanes(h)]

        def ahead(t):
            return lax.rem(me_a + t, n_a)

        def behind(t):
            return lax.rem(me_a - t + n_a, n_a)

        def to_right(t, h):
            ref = chunk(behind(t), h)
            return copy(ref, ref, r_send.at[2 * t + h], r_recv.at[2 * t + h], peer_a(1))

        def to_left(t, h):
            ref = chunk(ahead(t), h)
            return copy(ref, ref, l_send.at[2 * t + h], l_recv.at[2 * t + h], peer_a(n_a - 1))

        def to_twin(owner, h):
            ref = chunk(owner, h)
            return copy(ref, ref, t_send.at[2 * owner + h], t_recv.at[2 * owner + h], sibling)

        whole = (n_a - 1) // 2
        right_steps = [(t, h) for t in range(whole) for h in range(2)]
        left_steps = list(right_steps)
        if n_a % 2 == 0:
            right_steps.append((whole, 0))
            left_steps.append((whole, 1))
        for t in range(whole + 1):
            for h in range(2):
                if t == 0:
                    each(n_b, lambda k: fourth(k, h).wait())
                if (t, h) in right_steps:
                    if t > 0:
                        to_right(t - 1, h).wait_recv()
                    to_right(t, h).start()
                    if t > 0:
                        to_twin(behind(t), h).start()
                if (t, h) in left_steps:
                    if t > 0:
                        to_left(t - 1, h).wait_recv()
                    to_left(t, h).start()
                    if t > 0:
                        to_twin(ahead(t), h).start()
                if t == 0:
                    to_twin(me_a, h).start()
            if t == 0:
                est_ring.finish()
                for k in range(1, nx):
                    est_twin(k).start()
        for t, h in right_steps:
            if (t + 1, h) not in right_steps:
                to_right(t, h).wait_recv()
                to_twin(behind(t + 1), h).start()
        for t, h in left_steps:
            if (t + 1, h) not in left_steps:
                to_left(t, h).wait_recv()
                to_twin(ahead(t + 1), h).start()
        for t, h in right_steps:
            to_right(t, h).wait_send()
        for t, h in left_steps:
            to_left(t, h).wait_send()

        @pl.loop(0, 2 * other_n)
        def _(n):
            ref = cov_ref.at[
                :, 1 - c, pl.ds(pl.multiple_of(n // 2 * other_rows, 8), other_rows),
                pl.ds(pl.multiple_of(lax.rem(n, 2) * lane, lane), lane),
            ]
            copy(ref, ref, t_send.at[n], t_recv.at[n], sibling).wait_recv()

        @pl.loop(0, 2 * n_a)
        def _(n):
            ref = cov_ref.at[
                :, c, pl.ds(pl.multiple_of(n // 2 * rows_a, 8), rows_a),
                pl.ds(pl.multiple_of(lax.rem(n, 2) * lane, lane), lane),
            ]
            copy(ref, ref, t_send.at[n], t_recv.at[n], sibling).wait_send()

    @pl.when(c == 0)
    def _():
        reduce_and_gather(y, y_peer, ny, z, z_peer, nz, rows // nz, nz)

    @pl.when(c == 1)
    def _():
        reduce_and_gather(z, z_peer, nz, y, y_peer, ny, rows // ny, ny)

    est_local.wait()
    for k in range(1, nx):
        est_twin(k).wait()


def exchange(dims, sample_total, tab, own, estimate):
    nx, ny, nz = dims
    own_blocks, rows_dev, width = own.shape
    blocks = own_blocks * nx
    per_x = PAIRS // nx
    half = width // 2
    rows = per_x * half
    most = max(ny, nz)
    dma = pltpu.SemaphoreType.DMA
    f32 = jnp.float32
    smem = pl.BlockSpec(memory_space=pltpu.SMEM)
    vmem = pl.BlockSpec(memory_space=pltpu.VMEM)
    hbm = pl.BlockSpec(memory_space=pl.ANY)
    return pl.pallas_call(
        functools.partial(exchange_kernel, dims, sample_total),
        out_shape=(
            jax.ShapeDtypeStruct((nx, 2, rows, width), f32),
            jax.ShapeDtypeStruct((blocks,) + estimate.shape[1:], f32),
        ),
        in_specs=[smem, vmem, pl.BlockSpec(memory_space=pltpu.HBM)],
        out_specs=(hbm, hbm),
        scratch_shapes=[
            pltpu.VMEM((blocks, rows_dev, width), jnp.bfloat16),
            pltpu.VMEM((2, per_x, half, width), f32),
            pltpu.VMEM((per_x, half, width), f32),
            pltpu.VMEM((rows, width), f32),
            pltpu.VMEM((most - 1, rows // min(ny, nz), width), f32),
            pltpu.VMEM((rows // min(ny, nz), width), f32),
            pltpu.VMEM((most - 1, rows // (ny * nz), width), f32),
            pltpu.VMEM((rows // (ny * nz), width), f32),
            dma((6,)), dma((6,)),
            dma((per_x,)), dma((per_x,)),
            dma((2, most - 1)), dma((2, most - 1)),
            dma((2, most - 1)), dma((2, most - 1)),
            dma((2, nx - 1)), dma((2, nx - 1)),
            dma((2, most - 1)), dma((2, most - 1)),
            dma((2 * most,)), dma((2 * most,)),
            dma((2 * most,)), dma((2 * most,)),
            dma((2 * most,)), dma((2 * most,)),
            dma((6,)), dma((6,)),
            dma((nx - 1,)), dma((nx - 1,)),
            dma((3,)),
        ],
        compiler_params=pltpu.CompilerParams(
            collective_id=0, has_side_effects=True, vmem_limit_bytes=VMEM_EXCHANGE
        ),
    )(tab, own, estimate)


def steps_kernel(
    nx, tab, cov_ref, est_ref, out_ref,
    high, low, prec, weights, terms,
):
    blocks, stacked, width = est_ref.shape
    slots = stacked // width
    half = width // 2
    per_x = PAIRS // nx
    f32, bf16 = jnp.float32, jnp.bfloat16

    def row_of(j, s):
        return tab[TABLE + s * blocks + j]

    def count(j):
        return tab[COUNTS + j]

    def holder(q):
        return tab[HOLDER + q]

    def position(i):
        return tab[POSITION + i]

    def pair_of(a, b):
        listed = tab[RANK + jnp.minimum(a, b) * blocks + jnp.maximum(a, b)]
        return listed + jnp.where(a <= b, 0, PAIRS)

    @pl.loop(0, PAIRS)
    def _(t):
        @pl.when((t == 0) | (tab[RIGHT + t] > 0))
        def _():
            u = lax.rem(t, per_x)
            for h in range(2):
                value = cov_ref[t // per_x, h, pl.ds(pl.multiple_of(u * half, 8), half)]
                top = value.astype(bf16)
                high[t, h * half:(h + 1) * half] = top
                low[t, h * half:(h + 1) * half] = (value - top.astype(f32)).astype(bf16)

        @pl.when(tab[LEFT + t] != tab[RIGHT + t])
        def _():
            high[PAIRS + t] = high[t].T
            low[PAIRS + t] = low[t].T

    def block_of(q, s):
        return est_ref[q, pl.ds(pl.multiple_of(s * width, 8), width)]

    def mirror(j, i):
        return jnp.where(row_of(i, 0) == j, 0, jnp.where(row_of(i, 1) == j, 1, 2))

    def products(q, row_blocks, n, dests):
        j = holder(q)
        for i, dest in zip(row_blocks, dests):
            total = None
            for t in range(n):
                pair = pair_of(i, row_of(j, t))
                w = weights[q * slots + t]
                both = jnp.dot(high[pair], w, preferred_element_type=f32) + jnp.dot(
                    low[pair], w, preferred_element_type=f32
                )
                total = both if total is None else total + both
            terms[dest] = total

    def update(q, s, current):
        j = holder(q)
        i = row_of(j, s)
        other = position(i) * slots + mirror(j, i)
        gram = terms[q * slots + s] + terms[other].T
        stepped = current - (0.5 * step_size) * gram
        bound = step_size * penalty
        shrunk = jnp.maximum(stepped - bound, 0.0) + jnp.minimum(stepped + bound, 0.0)
        barrier = 0.5 * (stepped + jnp.sqrt(stepped * stepped + 4.0 * step_size))
        same = lax.broadcasted_iota(jnp.int32, (width, width), 0) == lax.broadcasted_iota(
            jnp.int32, (width, width), 1
        )
        return jnp.where(same & (i == j), barrier, shrunk)

    own_count, own_rows = out_ref.shape[0], out_ref.shape[1]
    own_slot = tab[PLACE + 1]
    first_row = tab[PLACE + 2]
    read = []
    for n in range(own_count):
        q = tab[PLACE] * own_count + n
        read += [q, position(row_of(holder(q), own_slot))]

    def is_read(q):
        return functools.reduce(jnp.logical_or, [q == other for other in read])

    def live_blocks(action, wanted=None):
        @pl.loop(0, blocks * slots)
        def _(flat):
            q, s = flat // slots, lax.rem(flat, slots)
            live = s < count(holder(q))

            @pl.when(live if wanted is None else live & wanted(q))
            def _():
                action(flat, q, s)

    def first_weights(flat, q, s):
        weights[flat] = block_of(q, s).astype(bf16)

    live_blocks(first_weights)

    for iteration in range(ITERS - 1):
        @pl.loop(0, blocks)
        def _(q):
            j = holder(q)
            whole = is_read(q)
            for n in range(1, slots + 1):
                @pl.when(whole & (count(j) == n))
                def _():
                    products(q, [row_of(j, s) for s in range(n)], n, [q * slots + s for s in range(n)])

                for s in range(1, n):
                    i = row_of(j, s)

                    @pl.when(jnp.logical_not(whole) & (count(j) == n) & is_read(position(i)))
                    def _():
                        products(q, [i], n, [q * slots + s])

        def renew(flat, q, s):
            value = update(q, s, block_of(q, s) if iteration == 0 else prec[flat])
            prec[flat] = value
            weights[flat] = value.astype(bf16)

        live_blocks(renew, is_read)

    s = own_slot

    def one_block(q, i, dest):
        for n in range(1, slots + 1):
            @pl.when(count(holder(q)) == n)
            def _():
                products(q, [i], n, [dest])

    for n in range(own_count):
        q = tab[PLACE] * own_count + n
        j = holder(q)
        live = s < count(j)

        @pl.when(live)
        def _():
            i = row_of(j, s)
            qi = position(i)
            one_block(q, i, q * slots + s)

            @pl.when(i != j)
            def _():
                one_block(qi, j, qi * slots + mirror(j, i))

            terms[q * slots + s] = update(q, s, prec[q * slots + s])
            if own_rows % 8 == 0:
                out_ref[n] = terms[q * slots + s, pl.ds(pl.multiple_of(first_row, 8), own_rows)]
            else:
                eight = terms[q * slots + s, pl.ds(pl.multiple_of(first_row // 8 * 8, 8), 8)]
                out_ref[n] = jnp.where(lax.rem(first_row, 8) == 0, eight[:own_rows], eight[8 - own_rows:])

        @pl.when(jnp.logical_not(live))
        def _():
            out_ref[n] = jnp.zeros(out_ref.shape[1:], f32)


def steps(nx, tab, cov, estimate, own_rows):
    blocks, stacked, width = estimate.shape
    count = blocks * (stacked // width)
    f32, bf16 = jnp.float32, jnp.bfloat16
    vmem = pl.BlockSpec(memory_space=pltpu.VMEM)
    smem = pl.BlockSpec(memory_space=pltpu.SMEM)
    return pl.pallas_call(
        functools.partial(steps_kernel, nx),
        out_shape=jax.ShapeDtypeStruct((blocks // nx, own_rows, width), f32),
        in_specs=[smem, vmem, vmem],
        out_specs=vmem,
        scratch_shapes=[
            pltpu.VMEM((2 * PAIRS, width, width), bf16),
            pltpu.VMEM((2 * PAIRS, width, width), bf16),
            pltpu.VMEM((count, width, width), f32),
            pltpu.VMEM((count, width, width), bf16),
            pltpu.VMEM((count, width, width), f32),
        ],
        compiler_params=pltpu.CompilerParams(vmem_limit_bytes=VMEM_STEPS),
    )(tab, cov, estimate)


def pair_tables(block_rows, counts):
    blocks, slots = block_rows.shape
    ids = jnp.arange(blocks, dtype=jnp.int32)
    live = jnp.arange(slots, dtype=jnp.int32)[None, :] < counts[:, None]
    has = jnp.any(live[:, :, None] & (block_rows[:, :, None] == ids), axis=1)
    need = jnp.any(has[:, :, None] & has[:, None, :], axis=0) & (ids[:, None] <= ids[None, :])
    flat = need.reshape(-1).astype(jnp.int32)
    order = jnp.arange(blocks * blocks, dtype=jnp.int32)
    rank = jnp.sum(jnp.where(order[None, :] < order[:, None], flat[None, :], 0), axis=1)
    hit = (flat[None, :] > 0) & (rank[None, :] == jnp.arange(PAIRS, dtype=jnp.int32)[:, None])
    which = jnp.sum(jnp.where(hit, order[None, :], 0), axis=1)
    return which // blocks, which % blocks, rank


def integer_table(block_rows, counts, holder, own_rows, width):
    blocks, slots = block_rows.shape
    raw = jnp.concatenate([block_rows[:, s] for s in range(slots)] + [counts, holder])
    raw = lax.optimization_barrier(raw)
    columns = raw.reshape(slots + 2, blocks)
    left, right, rank = pair_tables(columns[:slots].T, columns[slots])
    ids = jnp.arange(blocks, dtype=jnp.int32)
    position = jnp.sum(jnp.where(columns[slots + 1][:, None] == ids[None, :], ids[:, None], 0), axis=0)
    first = lax.axis_index("samp") * own_rows
    place = jnp.stack([lax.axis_index("var"), first // width, first % width]).astype(jnp.int32)
    return jnp.concatenate([raw, position, rank, left, right, place])


def body(dims, samples, estimate, block_rows, counts, holder):
    nx, ny, nz = dims
    rows_dev, _, width = samples.shape
    samp_count = 2 * ny * nz
    own_rows = block_rows.shape[1] * width // samp_count
    tab = integer_table(block_rows, counts, holder, own_rows, width)
    own = samples.transpose(1, 0, 2)
    cov, every = exchange(dims, rows_dev * samp_count, tab, own, estimate)
    return steps(nx, tab, cov, every, own_rows)


def solution(mesh):
    nx = mesh.shape["var"]
    ny, nz = (8, 12) if mesh.shape["samp"] == 192 else (2, 2)
    return jax.shard_map(
        functools.partial(body, (nx, ny, nz)),
        mesh=mesh,
        in_specs=(P("samp", "var", None), P("var", None, None), P(), P(), P()),
        out_specs=P("var", "samp", None),
        check_vma=False,
    )
```

```python
import functools

import jax
import jax.numpy as jnp
from jax import lax
from jax.experimental import pallas as pl
from jax.experimental.pallas import tpu as pltpu
from jax.sharding import PartitionSpec as P

MESH = pl.DeviceIdType.MESH
ITERS = 2
PAIRS = 24
VMEM_EXCHANGE = 12 << 20
VMEM_STEPS = 34 << 20

TABLE, COUNTS, HOLDER, POSITION, RANK, LEFT, RIGHT, PLACE = 0, 24, 32, 40, 48, 112, 136, 160
step_size = 0.1
penalty = 5.0


def exchange_kernel(
    dims, sample_total, tab, own_ref, est_ref, cov_ref, all_ref,
    data, part, twin, acc, got1, mid, got2, share,
    x_send, x_recv, d_send, d_recv, s1_send, s1_recv, s2_send, s2_recv,
    e_send, e_recv, b_send, b_recv, r_send, r_recv, l_send, l_recv,
    t_send, t_recv, p_send, p_recv, pd_send, pd_recv, loc_sem,
):
    nx, ny, nz = dims
    s = lax.axis_index("samp")
    x = lax.axis_index("var")
    c = lax.rem(s, 2)
    z = lax.rem(s // 2, nz)
    y = s // (2 * nz)
    own_blocks = own_ref.shape[0]
    per_x = PAIRS // nx
    rows = acc.shape[0]
    half = rows // per_x

    def at(xx, yy, zz, cc):
        return ((yy * nz + zz) * 2 + cc, xx)

    def x_peer(k):
        return at(lax.rem(x + k, nx), y, z, c)

    def y_peer(k):
        return at(x, lax.rem(y + k, ny), z, c)

    def z_peer(k):
        return at(x, y, lax.rem(z + k, nz), c)

    sibling = at(x, y, z, 1 - c)

    def copy(src, dst, send, recv, device):
        return pltpu.make_async_remote_copy(
            src_ref=src, dst_ref=dst, send_sem=send, recv_sem=recv, device_id=device, device_id_type=MESH
        )

    barrier = pltpu.get_barrier_semaphore()
    for peer, n in ((x_peer, nx), (y_peer, ny), (z_peer, nz)):
        @pl.loop(1, n)
        def _(k, peer=peer):
            pl.semaphore_signal(barrier, inc=1, device_id=peer(k), device_id_type=MESH)
    pl.semaphore_signal(barrier, inc=1, device_id=sibling, device_id_type=MESH)
    pl.semaphore_wait(barrier, nx + ny + nz - 2)

    class Ring:
        def __init__(self, own_piece, piece, send, recv):
            right, left = lax.rem(x + 1, nx), lax.rem(x + nx - 1, nx)

            def to(k, owner, n, sem):
                src = own_piece(n) if owner is None else piece(owner, n)
                dst = piece(x if owner is None else owner, n)
                return copy(src, dst, send.at[sem], recv.at[sem], x_peer(k))

            self.own = [to(1, None, 0, 0), to(nx - 1, None, 1, 1), to(1, None, 1, 2), to(nx - 1, None, 0, 3)]
            self.onward = [to(1, left, 0, 4), to(nx - 1, right, 1, 5)]

        def start(self):
            for cp in self.own:
                cp.start()

        def forward(self):
            for n in range(2):
                self.own[n].wait_recv()
                self.onward[n].start()

        def finish(self):
            self.own[2].wait_recv()
            self.own[3].wait_recv()
            for cp in self.onward:
                cp.wait_recv()
            for cp in self.own + self.onward:
                cp.wait_send()

    mine = pl.ds(x * own_blocks, own_blocks)
    samples_ring = Ring(
        lambda n: own_ref.at[n], lambda owner, n: data.at[owner * own_blocks + n], x_send, x_recv
    )
    samples_ring.start()
    est_local = pltpu.make_async_copy(est_ref, all_ref.at[mine], loc_sem.at[0])
    est_local.start()
    data[mine] = own_ref[...]
    samples_ring.forward()
    samples_ring.finish()

    est_half = est_ref.shape[1] // 2

    def est_rows(n):
        return pl.ds(n * est_half, est_half)

    est_ring = Ring(
        lambda n: est_ref.at[c, est_rows(n)],
        lambda owner, n: all_ref.at[owner * own_blocks + c, est_rows(n)],
        p_send, p_recv,
    )
    est_ring.start()

    pair_copies = []
    for u in range(per_x):
        left = data[tab[LEFT + x * per_x + u]]
        right = data[tab[RIGHT + x * per_x + u]]
        prod = lax.dot_general(left, right, (((0,), (0,)), ((), ())), preferred_element_type=jnp.float32)
        part[0, u] = prod[:half]
        part[1, u] = prod[half:]
        cp = copy(part.at[1 - c, u], twin.at[u], d_send.at[u], d_recv.at[u], sibling)
        cp.start()
        pair_copies.append(cp)
    for u in range(per_x):
        pair_copies[u].wait()
        acc[u * half:(u + 1) * half] = part[c, u] + twin[u]

    def est_twin(k):
        ref = all_ref.at[lax.rem(x + k, nx) * own_blocks + c]
        return copy(ref, ref, pd_send.at[k - 1], pd_recv.at[k - 1], sibling)

    lane = own_ref.shape[2] // 2

    def lanes(g):
        return pl.ds(g * lane, lane)

    def reduce_and_gather(me_a, peer_a, n_a, me_b, peer_b, n_b, other_rows, other_n):
        rows_a = rows // n_a
        rows_b = rows_a // n_b
        groups = range(2)

        def each(n, action):
            @pl.loop(1, n)
            def _(k):
                action(k)

        def first(k, g):
            return copy(
                acc.at[pl.ds(lax.rem(me_a + k, n_a) * rows_a, rows_a), lanes(g)],
                got1.at[k - 1, pl.ds(0, rows_a), lanes(g)],
                s1_send.at[g, k - 1], s1_recv.at[g, k - 1], peer_a(k),
            )

        def second(k, g):
            return copy(
                mid.at[pl.ds(lax.rem(me_b + k, n_b) * rows_b, rows_b), lanes(g)], got2.at[k - 1, :, lanes(g)],
                s2_send.at[g, k - 1], s2_recv.at[g, k - 1], peer_b(k),
            )

        first_row = pl.multiple_of(me_a * rows_a + me_b * rows_b, 8)
        place = pl.ds(first_row, rows_b)

        def third(k, g):
            return copy(
                share.at[:, lanes(g)], cov_ref.at[x, c, place, lanes(g)],
                b_send.at[g, k - 1], b_recv.at[g, k - 1], peer_b(k),
            )

        def fourth(k, g):
            ref = cov_ref.at[x, c, pl.ds(pl.multiple_of(me_a * rows_a, 8), rows_a), lanes(g)]
            return copy(ref, ref, e_send.at[g, k - 1], e_recv.at[g, k - 1], x_peer(k))

        for g in groups:
            each(n_a, lambda k: first(k, g).start())
        est_ring.forward()
        for g in groups:
            here = slice(g * lane, (g + 1) * lane)
            mid[pl.ds(0, rows_a), here] = acc[pl.ds(pl.multiple_of(me_a * rows_a, 8), rows_a), here]

            def add_first(k):
                first(k, g).wait()
                mid[pl.ds(0, rows_a), here] += got1[k - 1, pl.ds(0, rows_a), here]

            each(n_a, add_first)
            each(n_b, lambda k: second(k, g).start())
        for g in groups:
            here = slice(g * lane, (g + 1) * lane)
            share[:, here] = mid[pl.ds(pl.multiple_of(me_b * rows_b, 8), rows_b), here]

            def add_second(k):
                second(k, g).wait()
                share[:, here] += got2[k - 1, :, here]

            each(n_b, add_second)
            share[:, here] = share[:, here] * (1.0 / sample_total)
            each(n_b, lambda k: third(k, g).start())
            own_share = pltpu.make_async_copy(
                share.at[:, lanes(g)], cov_ref.at[x, c, place, lanes(g)], loc_sem.at[1 + g]
            )
            own_share.start()
            own_share.wait()
        for g in groups:
            each(n_b, lambda k: third(k, g).wait())
            each(nx, lambda k: fourth(k, g).start())

        def chunk(owner, h):
            return cov_ref.at[:, c, pl.ds(pl.multiple_of(owner * rows_a, 8), rows_a), lanes(h)]

        def ahead(t):
            return lax.rem(me_a + t, n_a)

        def behind(t):
            return lax.rem(me_a - t + n_a, n_a)

        def to_right(t, h):
            ref = chunk(behind(t), h)
            return copy(ref, ref, r_send.at[2 * t + h], r_recv.at[2 * t + h], peer_a(1))

        def to_left(t, h):
            ref = chunk(ahead(t), h)
            return copy(ref, ref, l_send.at[2 * t + h], l_recv.at[2 * t + h], peer_a(n_a - 1))

        def to_twin(owner, h):
            ref = chunk(owner, h)
            return copy(ref, ref, t_send.at[2 * owner + h], t_recv.at[2 * owner + h], sibling)

        whole = (n_a - 1) // 2
        right_steps = [(t, h) for t in range(whole) for h in range(2)]
        left_steps = list(right_steps)
        if n_a % 2 == 0:
            right_steps.append((whole, 0))
            left_steps.append((whole, 1))
        for t in range(whole + 1):
            for h in range(2):
                if t == 0:
                    each(nx, lambda k: fourth(k, h).wait())
                if (t, h) in right_steps:
                    if t > 0:
                        to_right(t - 1, h).wait_recv()
                    to_right(t, h).start()
                    if t > 0:
                        to_twin(behind(t), h).start()
                if (t, h) in left_steps:
                    if t > 0:
                        to_left(t - 1, h).wait_recv()
                    to_left(t, h).start()
                    if t > 0:
                        to_twin(ahead(t), h).start()
                if t == 0:
                    to_twin(me_a, h).start()
            if t == 0:
                est_ring.finish()
                for k in range(1, nx):
                    est_twin(k).start()
        for t, h in right_steps:
            if (t + 1, h) not in right_steps:
                to_right(t, h).wait_recv()
                to_twin(behind(t + 1), h).start()
        for t, h in left_steps:
            if (t + 1, h) not in left_steps:
                to_left(t, h).wait_recv()
                to_twin(ahead(t + 1), h).start()
        for t, h in right_steps:
            to_right(t, h).wait_send()
        for t, h in left_steps:
            to_left(t, h).wait_send()

        @pl.loop(0, 2 * other_n)
        def _(n):
            ref = cov_ref.at[
                :, 1 - c, pl.ds(pl.multiple_of(n // 2 * other_rows, 8), other_rows),
                pl.ds(pl.multiple_of(lax.rem(n, 2) * lane, lane), lane),
            ]
            copy(ref, ref, t_send.at[n], t_recv.at[n], sibling).wait_recv()

        @pl.loop(0, 2 * n_a)
        def _(n):
            ref = cov_ref.at[
                :, c, pl.ds(pl.multiple_of(n // 2 * rows_a, 8), rows_a),
                pl.ds(pl.multiple_of(lax.rem(n, 2) * lane, lane), lane),
            ]
            copy(ref, ref, t_send.at[n], t_recv.at[n], sibling).wait_send()

    @pl.when(c == 0)
    def _():
        reduce_and_gather(y, y_peer, ny, z, z_peer, nz, rows // nz, nz)

    @pl.when(c == 1)
    def _():
        reduce_and_gather(z, z_peer, nz, y, y_peer, ny, rows // ny, ny)

    est_local.wait()
    for k in range(1, nx):
        est_twin(k).wait()


def exchange(dims, sample_total, tab, own, estimate):
    nx, ny, nz = dims
    own_blocks, rows_dev, width = own.shape
    blocks = own_blocks * nx
    per_x = PAIRS // nx
    half = width // 2
    rows = per_x * half
    most = max(ny, nz)
    dma = pltpu.SemaphoreType.DMA
    f32 = jnp.float32
    smem = pl.BlockSpec(memory_space=pltpu.SMEM)
    vmem = pl.BlockSpec(memory_space=pltpu.VMEM)
    hbm = pl.BlockSpec(memory_space=pl.ANY)
    return pl.pallas_call(
        functools.partial(exchange_kernel, dims, sample_total),
        out_shape=(
            jax.ShapeDtypeStruct((nx, 2, rows, width), f32),
            jax.ShapeDtypeStruct((blocks,) + estimate.shape[1:], f32),
        ),
        in_specs=[smem, vmem, pl.BlockSpec(memory_space=pltpu.HBM)],
        out_specs=(hbm, hbm),
        scratch_shapes=[
            pltpu.VMEM((blocks, rows_dev, width), jnp.bfloat16),
            pltpu.VMEM((2, per_x, half, width), f32),
            pltpu.VMEM((per_x, half, width), f32),
            pltpu.VMEM((rows, width), f32),
            pltpu.VMEM((most - 1, rows // min(ny, nz), width), f32),
            pltpu.VMEM((rows // min(ny, nz), width), f32),
            pltpu.VMEM((most - 1, rows // (ny * nz), width), f32),
            pltpu.VMEM((rows // (ny * nz), width), f32),
            dma((6,)), dma((6,)),
            dma((per_x,)), dma((per_x,)),
            dma((2, most - 1)), dma((2, most - 1)),
            dma((2, most - 1)), dma((2, most - 1)),
            dma((2, nx - 1)), dma((2, nx - 1)),
            dma((2, most - 1)), dma((2, most - 1)),
            dma((2 * most,)), dma((2 * most,)),
            dma((2 * most,)), dma((2 * most,)),
            dma((2 * most,)), dma((2 * most,)),
            dma((6,)), dma((6,)),
            dma((nx - 1,)), dma((nx - 1,)),
            dma((3,)),
        ],
        compiler_params=pltpu.CompilerParams(
            collective_id=0, has_side_effects=True, vmem_limit_bytes=VMEM_EXCHANGE
        ),
    )(tab, own, estimate)


def steps_kernel(
    nx, tab, cov_ref, est_ref, out_ref,
    high, low, prec, weights, terms,
):
    blocks, stacked, width = est_ref.shape
    slots = stacked // width
    half = width // 2
    per_x = PAIRS // nx
    f32, bf16 = jnp.float32, jnp.bfloat16

    def row_of(j, s):
        return tab[TABLE + s * blocks + j]

    def count(j):
        return tab[COUNTS + j]

    def holder(q):
        return tab[HOLDER + q]

    def position(i):
        return tab[POSITION + i]

    def pair_of(a, b):
        listed = tab[RANK + jnp.minimum(a, b) * blocks + jnp.maximum(a, b)]
        return listed + jnp.where(a <= b, 0, PAIRS)

    @pl.loop(0, PAIRS)
    def _(t):
        @pl.when((t == 0) | (tab[RIGHT + t] > 0))
        def _():
            u = lax.rem(t, per_x)
            for h in range(2):
                value = cov_ref[t // per_x, h, pl.ds(pl.multiple_of(u * half, 8), half)]
                top = value.astype(bf16)
                high[t, h * half:(h + 1) * half] = top
                low[t, h * half:(h + 1) * half] = (value - top.astype(f32)).astype(bf16)

        @pl.when(tab[LEFT + t] != tab[RIGHT + t])
        def _():
            high[PAIRS + t] = high[t].T
            low[PAIRS + t] = low[t].T

    def block_of(q, s):
        return est_ref[q, pl.ds(pl.multiple_of(s * width, 8), width)]

    def mirror(j, i):
        return jnp.where(row_of(i, 0) == j, 0, jnp.where(row_of(i, 1) == j, 1, 2))

    def products(q, row_blocks, n, dests):
        j = holder(q)
        for i, dest in zip(row_blocks, dests):
            total = None
            for t in range(n):
                pair = pair_of(i, row_of(j, t))
                w = weights[q * slots + t]
                both = jnp.dot(high[pair], w, preferred_element_type=f32) + jnp.dot(
                    low[pair], w, preferred_element_type=f32
                )
                total = both if total is None else total + both
            terms[dest] = total

    def update(q, s, current):
        j = holder(q)
        i = row_of(j, s)
        other = position(i) * slots + mirror(j, i)
        gram = terms[q * slots + s] + terms[other].T
        stepped = current - (0.5 * step_size) * gram
        bound = step_size * penalty
        shrunk = jnp.maximum(stepped - bound, 0.0) + jnp.minimum(stepped + bound, 0.0)
        barrier = 0.5 * (stepped + jnp.sqrt(stepped * stepped + 4.0 * step_size))
        same = lax.broadcasted_iota(jnp.int32, (width, width), 0) == lax.broadcasted_iota(
            jnp.int32, (width, width), 1
        )
        return jnp.where(same & (i == j), barrier, shrunk)

    own_count, own_rows = out_ref.shape[0], out_ref.shape[1]
    own_slot = tab[PLACE + 1]
    first_row = tab[PLACE + 2]
    read = []
    for n in range(own_count):
        q = tab[PLACE] * own_count + n
        read += [q, position(row_of(holder(q), own_slot))]

    def is_read(q):
        return functools.reduce(jnp.logical_or, [q == other for other in read])

    def live_blocks(action, wanted=None):
        @pl.loop(0, blocks * slots)
        def _(flat):
            q, s = flat // slots, lax.rem(flat, slots)
            live = s < count(holder(q))

            @pl.when(live if wanted is None else live & wanted(q))
            def _():
                action(flat, q, s)

    def first_weights(flat, q, s):
        weights[flat] = block_of(q, s).astype(bf16)

    live_blocks(first_weights)

    for iteration in range(ITERS - 1):
        @pl.loop(0, blocks)
        def _(q):
            j = holder(q)
            whole = is_read(q)
            for n in range(1, slots + 1):
                @pl.when(whole & (count(j) == n))
                def _():
                    products(q, [row_of(j, s) for s in range(n)], n, [q * slots + s for s in range(n)])

                for s in range(1, n):
                    i = row_of(j, s)

                    @pl.when(jnp.logical_not(whole) & (count(j) == n) & is_read(position(i)))
                    def _():
                        products(q, [i], n, [q * slots + s])

        def renew(flat, q, s):
            value = update(q, s, block_of(q, s) if iteration == 0 else prec[flat])
            prec[flat] = value
            weights[flat] = value.astype(bf16)

        live_blocks(renew, is_read)

    s = own_slot

    def one_block(q, i, dest):
        for n in range(1, slots + 1):
            @pl.when(count(holder(q)) == n)
            def _():
                products(q, [i], n, [dest])

    for n in range(own_count):
        q = tab[PLACE] * own_count + n
        j = holder(q)
        live = s < count(j)

        @pl.when(live)
        def _():
            i = row_of(j, s)
            qi = position(i)
            one_block(q, i, q * slots + s)

            @pl.when(i != j)
            def _():
                one_block(qi, j, qi * slots + mirror(j, i))

            terms[q * slots + s] = update(q, s, prec[q * slots + s])
            if own_rows % 8 == 0:
                out_ref[n] = terms[q * slots + s, pl.ds(pl.multiple_of(first_row, 8), own_rows)]
            else:
                eight = terms[q * slots + s, pl.ds(pl.multiple_of(first_row // 8 * 8, 8), 8)]
                out_ref[n] = jnp.where(lax.rem(first_row, 8) == 0, eight[:own_rows], eight[8 - own_rows:])

        @pl.when(jnp.logical_not(live))
        def _():
            out_ref[n] = jnp.zeros(out_ref.shape[1:], f32)


def steps(nx, tab, cov, estimate, own_rows):
    blocks, stacked, width = estimate.shape
    count = blocks * (stacked // width)
    f32, bf16 = jnp.float32, jnp.bfloat16
    vmem = pl.BlockSpec(memory_space=pltpu.VMEM)
    smem = pl.BlockSpec(memory_space=pltpu.SMEM)
    return pl.pallas_call(
        functools.partial(steps_kernel, nx),
        out_shape=jax.ShapeDtypeStruct((blocks // nx, own_rows, width), f32),
        in_specs=[smem, vmem, vmem],
        out_specs=vmem,
        scratch_shapes=[
            pltpu.VMEM((2 * PAIRS, width, width), bf16),
            pltpu.VMEM((2 * PAIRS, width, width), bf16),
            pltpu.VMEM((count, width, width), f32),
            pltpu.VMEM((count, width, width), bf16),
            pltpu.VMEM((count, width, width), f32),
        ],
        compiler_params=pltpu.CompilerParams(vmem_limit_bytes=VMEM_STEPS),
    )(tab, cov, estimate)


def pair_tables(block_rows, counts):
    blocks, slots = block_rows.shape
    ids = jnp.arange(blocks, dtype=jnp.int32)
    live = jnp.arange(slots, dtype=jnp.int32)[None, :] < counts[:, None]
    has = jnp.any(live[:, :, None] & (block_rows[:, :, None] == ids), axis=1)
    need = jnp.any(has[:, :, None] & has[:, None, :], axis=0) & (ids[:, None] <= ids[None, :])
    flat = need.reshape(-1).astype(jnp.int32)
    order = jnp.arange(blocks * blocks, dtype=jnp.int32)
    rank = jnp.sum(jnp.where(order[None, :] < order[:, None], flat[None, :], 0), axis=1)
    hit = (flat[None, :] > 0) & (rank[None, :] == jnp.arange(PAIRS, dtype=jnp.int32)[:, None])
    which = jnp.sum(jnp.where(hit, order[None, :], 0), axis=1)
    return which // blocks, which % blocks, rank


def integer_table(block_rows, counts, holder, own_rows, width):
    blocks, slots = block_rows.shape
    raw = jnp.concatenate([block_rows[:, s] for s in range(slots)] + [counts, holder])
    raw = lax.optimization_barrier(raw)
    columns = raw.reshape(slots + 2, blocks)
    left, right, rank = pair_tables(columns[:slots].T, columns[slots])
    ids = jnp.arange(blocks, dtype=jnp.int32)
    position = jnp.sum(jnp.where(columns[slots + 1][:, None] == ids[None, :], ids[:, None], 0), axis=0)
    first = lax.axis_index("samp") * own_rows
    place = jnp.stack([lax.axis_index("var"), first // width, first % width]).astype(jnp.int32)
    return jnp.concatenate([raw, position, rank, left, right, place])


def body(dims, samples, estimate, block_rows, counts, holder):
    nx, ny, nz = dims
    rows_dev, _, width = samples.shape
    samp_count = 2 * ny * nz
    own_rows = block_rows.shape[1] * width // samp_count
    tab = integer_table(block_rows, counts, holder, own_rows, width)
    own = samples.transpose(1, 0, 2)
    cov, every = exchange(dims, rows_dev * samp_count, tab, own, estimate)
    return steps(nx, tab, cov, every, own_rows)


def solution(mesh):
    nx = mesh.shape["var"]
    ny, nz = (8, 12) if mesh.shape["samp"] == 192 else (2, 2)
    return jax.shard_map(
        functools.partial(body, (nx, ny, nz)),
        mesh=mesh,
        in_specs=(P("samp", "var", None), P("var", None, None), P(), P(), P()),
        out_specs=P("var", "samp", None),
        check_vma=False,
    )
```

```python
import functools

import jax
import jax.numpy as jnp
from jax import lax
from jax.experimental import pallas as pl
from jax.experimental.pallas import tpu as pltpu
from jax.sharding import PartitionSpec as P

MESH = pl.DeviceIdType.MESH
ITERS = 2
PAIRS = 24
VMEM_EXCHANGE = 12 << 20
VMEM_STEPS = 34 << 20

TABLE, COUNTS, HOLDER, POSITION, RANK, LEFT, RIGHT, PLACE = 0, 24, 32, 40, 48, 112, 136, 160
step_size = 0.1
penalty = 5.0


def exchange_kernel(
    dims, sample_total, tab, own_ref, est_ref, cov_ref, all_ref,
    data, part, twin, acc, got1, mid, got2, share,
    x_send, x_recv, d_send, d_recv, s1_send, s1_recv, s2_send, s2_recv,
    e_send, e_recv, b_send, b_recv, r_send, r_recv, l_send, l_recv,
    t_send, t_recv, p_send, p_recv, pd_send, pd_recv, loc_sem,
):
    nx, ny, nz = dims
    s = lax.axis_index("samp")
    x = lax.axis_index("var")
    c = lax.rem(s, 2)
    z = lax.rem(s // 2, nz)
    y = s // (2 * nz)
    own_blocks = own_ref.shape[0]
    per_x = PAIRS // nx
    rows = acc.shape[0]
    half = rows // per_x

    def at(xx, yy, zz, cc):
        return ((yy * nz + zz) * 2 + cc, xx)

    def x_peer(k):
        return at(lax.rem(x + k, nx), y, z, c)

    def y_peer(k):
        return at(x, lax.rem(y + k, ny), z, c)

    def z_peer(k):
        return at(x, y, lax.rem(z + k, nz), c)

    sibling = at(x, y, z, 1 - c)

    def copy(src, dst, send, recv, device):
        return pltpu.make_async_remote_copy(
            src_ref=src, dst_ref=dst, send_sem=send, recv_sem=recv, device_id=device, device_id_type=MESH
        )

    barrier = pltpu.get_barrier_semaphore()
    for peer, n in ((x_peer, nx), (y_peer, ny), (z_peer, nz)):
        @pl.loop(1, n)
        def _(k, peer=peer):
            pl.semaphore_signal(barrier, inc=1, device_id=peer(k), device_id_type=MESH)
    pl.semaphore_signal(barrier, inc=1, device_id=sibling, device_id_type=MESH)
    pl.semaphore_wait(barrier, nx + ny + nz - 2)

    class Ring:
        def __init__(self, own_piece, piece, send, recv):
            right, left = lax.rem(x + 1, nx), lax.rem(x + nx - 1, nx)

            def to(k, owner, n, sem):
                src = own_piece(n) if owner is None else piece(owner, n)
                dst = piece(x if owner is None else owner, n)
                return copy(src, dst, send.at[sem], recv.at[sem], x_peer(k))

            self.own = [to(1, None, 0, 0), to(nx - 1, None, 1, 1), to(1, None, 1, 2), to(nx - 1, None, 0, 3)]
            self.onward = [to(1, left, 0, 4), to(nx - 1, right, 1, 5)]

        def start(self):
            for cp in self.own:
                cp.start()

        def forward(self):
            for n in range(2):
                self.own[n].wait_recv()
                self.onward[n].start()

        def finish(self):
            self.own[2].wait_recv()
            self.own[3].wait_recv()
            for cp in self.onward:
                cp.wait_recv()
            for cp in self.own + self.onward:
                cp.wait_send()

    mine = pl.ds(x * own_blocks, own_blocks)
    samples_ring = Ring(
        lambda n: own_ref.at[n], lambda owner, n: data.at[owner * own_blocks + n], x_send, x_recv
    )
    samples_ring.start()
    est_local = pltpu.make_async_copy(est_ref, all_ref.at[mine], loc_sem.at[0])
    est_local.start()
    data[mine] = own_ref[...]
    samples_ring.forward()
    samples_ring.finish()

    est_half = est_ref.shape[1] // 2

    def est_rows(n):
        return pl.ds(n * est_half, est_half)

    est_ring = Ring(
        lambda n: est_ref.at[c, est_rows(n)],
        lambda owner, n: all_ref.at[owner * own_blocks + c, est_rows(n)],
        p_send, p_recv,
    )
    est_ring.start()

    pair_copies = []
    for u in range(per_x):
        left = data[tab[LEFT + x * per_x + u]]
        right = data[tab[RIGHT + x * per_x + u]]
        prod = lax.dot_general(left, right, (((0,), (0,)), ((), ())), preferred_element_type=jnp.float32)
        part[0, u] = prod[:half]
        part[1, u] = prod[half:]
        cp = copy(part.at[1 - c, u], twin.at[u], d_send.at[u], d_recv.at[u], sibling)
        cp.start()
        pair_copies.append(cp)
    for u in range(per_x):
        pair_copies[u].wait()
        acc[u * half:(u + 1) * half] = part[c, u] + twin[u]

    def est_twin(k):
        ref = all_ref.at[lax.rem(x + k, nx) * own_blocks + c]
        return copy(ref, ref, pd_send.at[k - 1], pd_recv.at[k - 1], sibling)

    lane = own_ref.shape[2] // 2

    def lanes(g):
        return pl.ds(g * lane, lane)

    def reduce_and_gather(me_a, peer_a, n_a, me_b, peer_b, n_b, other_rows, other_n):
        rows_a = rows // n_a
        rows_b = rows_a // n_b
        groups = range(2)

        def each(n, action):
            @pl.loop(1, n)
            def _(k):
                action(k)

        def first(k, g):
            return copy(
                acc.at[pl.ds(lax.rem(me_a + k, n_a) * rows_a, rows_a), lanes(g)],
                got1.at[k - 1, pl.ds(0, rows_a), lanes(g)],
                s1_send.at[g, k - 1], s1_recv.at[g, k - 1], peer_a(k),
            )

        def second(k, g):
            return copy(
                mid.at[pl.ds(lax.rem(me_b + k, n_b) * rows_b, rows_b), lanes(g)], got2.at[k - 1, :, lanes(g)],
                s2_send.at[g, k - 1], s2_recv.at[g, k - 1], peer_b(k),
            )

        first_row = pl.multiple_of(me_a * rows_a + me_b * rows_b, 8)
        place = pl.ds(first_row, rows_b)

        def third(k, g):
            return copy(
                share.at[:, lanes(g)], cov_ref.at[x, c, place, lanes(g)],
                b_send.at[g, k - 1], b_recv.at[g, k - 1], peer_b(k),
            )

        def fourth(k, g):
            ref = cov_ref.at[x, c, pl.ds(pl.multiple_of(me_a * rows_a, 8), rows_a), lanes(g)]
            return copy(ref, ref, e_send.at[g, k - 1], e_recv.at[g, k - 1], x_peer(k))

        for g in groups:
            each(n_a, lambda k: first(k, g).start())
        est_ring.forward()
        for g in groups:
            here = slice(g * lane, (g + 1) * lane)
            mid[pl.ds(0, rows_a), here] = acc[pl.ds(pl.multiple_of(me_a * rows_a, 8), rows_a), here]

            def add_first(k):
                first(k, g).wait()
                mid[pl.ds(0, rows_a), here] += got1[k - 1, pl.ds(0, rows_a), here]

            each(n_a, add_first)
            each(n_b, lambda k: second(k, g).start())
        for g in groups:
            here = slice(g * lane, (g + 1) * lane)
            share[:, here] = mid[pl.ds(pl.multiple_of(me_b * rows_b, 8), rows_b), here]

            def add_second(k):
                second(k, g).wait()
                share[:, here] += got2[k - 1, :, here]

            each(n_b, add_second)
            share[:, here] = share[:, here] * (1.0 / sample_total)
            each(n_b, lambda k: third(k, g).start())
            own_share = pltpu.make_async_copy(
                share.at[:, lanes(g)], cov_ref.at[x, c, place, lanes(g)], loc_sem.at[1 + g]
            )
            own_share.start()
            own_share.wait()
        for g in groups:
            each(n_b, lambda k: third(k, g).wait())
            each(nx, lambda k: fourth(k, g).start())

        def chunk(owner, h):
            return cov_ref.at[:, c, pl.ds(pl.multiple_of(owner * rows_a, 8), rows_a), lanes(h)]

        def ahead(t):
            return lax.rem(me_a + t, n_a)

        def behind(t):
            return lax.rem(me_a - t + n_a, n_a)

        def to_right(t, h):
            ref = chunk(behind(t), h)
            return copy(ref, ref, r_send.at[2 * t + h], r_recv.at[2 * t + h], peer_a(1))

        def to_left(t, h):
            ref = chunk(ahead(t), h)
            return copy(ref, ref, l_send.at[2 * t + h], l_recv.at[2 * t + h], peer_a(n_a - 1))

        def to_twin(owner, h):
            ref = chunk(owner, h)
            return copy(ref, ref, t_send.at[2 * owner + h], t_recv.at[2 * owner + h], sibling)

        whole = (n_a - 1) // 2
        right_steps = [(t, h) for t in range(whole) for h in range(2)]
        left_steps = list(right_steps)
        if n_a % 2 == 0:
            right_steps.append((whole, 0))
            left_steps.append((whole, 1))
        for t in range(whole + 1):
            for h in range(2):
                if t == 0:
                    each(nx, lambda k: fourth(k, h).wait())
                if (t, h) in right_steps:
                    if t > 0:
                        to_right(t - 1, h).wait_recv()
                    to_right(t, h).start()
                    if t > 0:
                        to_twin(behind(t), h).start()
                if (t, h) in left_steps:
                    if t > 0:
                        to_left(t - 1, h).wait_recv()
                    to_left(t, h).start()
                    if t > 0:
                        to_twin(ahead(t), h).start()
                if t == 0:
                    to_twin(me_a, h).start()
            if t == 0:
                est_ring.finish()
                for k in range(1, nx):
                    est_twin(k).start()
        for t, h in right_steps:
            if (t + 1, h) not in right_steps:
                to_right(t, h).wait_recv()
                to_twin(behind(t + 1), h).start()
        for t, h in left_steps:
            if (t + 1, h) not in left_steps:
                to_left(t, h).wait_recv()
                to_twin(ahead(t + 1), h).start()
        for t, h in right_steps:
            to_right(t, h).wait_send()
        for t, h in left_steps:
            to_left(t, h).wait_send()

        @pl.loop(0, 2 * other_n)
        def _(n):
            ref = cov_ref.at[
                :, 1 - c, pl.ds(pl.multiple_of(n // 2 * other_rows, 8), other_rows),
                pl.ds(pl.multiple_of(lax.rem(n, 2) * lane, lane), lane),
            ]
            copy(ref, ref, t_send.at[n], t_recv.at[n], sibling).wait_recv()

        @pl.loop(0, 2 * n_a)
        def _(n):
            ref = cov_ref.at[
                :, c, pl.ds(pl.multiple_of(n // 2 * rows_a, 8), rows_a),
                pl.ds(pl.multiple_of(lax.rem(n, 2) * lane, lane), lane),
            ]
            copy(ref, ref, t_send.at[n], t_recv.at[n], sibling).wait_send()

    @pl.when(c == 0)
    def _():
        reduce_and_gather(y, y_peer, ny, z, z_peer, nz, rows // nz, nz)

    @pl.when(c == 1)
    def _():
        reduce_and_gather(z, z_peer, nz, y, y_peer, ny, rows // ny, ny)

    est_local.wait()
    for k in range(1, nx):
        est_twin(k).wait()


def exchange(dims, sample_total, tab, own, estimate):
    nx, ny, nz = dims
    own_blocks, rows_dev, width = own.shape
    blocks = own_blocks * nx
    per_x = PAIRS // nx
    half = width // 2
    rows = per_x * half
    most = max(ny, nz)
    dma = pltpu.SemaphoreType.DMA
    f32 = jnp.float32
    smem = pl.BlockSpec(memory_space=pltpu.SMEM)
    vmem = pl.BlockSpec(memory_space=pltpu.VMEM)
    hbm = pl.BlockSpec(memory_space=pl.ANY)
    return pl.pallas_call(
        functools.partial(exchange_kernel, dims, sample_total),
        out_shape=(
            jax.ShapeDtypeStruct((nx, 2, rows, width), f32),
            jax.ShapeDtypeStruct((blocks,) + estimate.shape[1:], f32),
        ),
        in_specs=[smem, vmem, pl.BlockSpec(memory_space=pltpu.HBM)],
        out_specs=(hbm, hbm),
        scratch_shapes=[
            pltpu.VMEM((blocks, rows_dev, width), jnp.bfloat16),
            pltpu.VMEM((2, per_x, half, width), f32),
            pltpu.VMEM((per_x, half, width), f32),
            pltpu.VMEM((rows, width), f32),
            pltpu.VMEM((most - 1, rows // min(ny, nz), width), f32),
            pltpu.VMEM((rows // min(ny, nz), width), f32),
            pltpu.VMEM((most - 1, rows // (ny * nz), width), f32),
            pltpu.VMEM((rows // (ny * nz), width), f32),
            dma((6,)), dma((6,)),
            dma((per_x,)), dma((per_x,)),
            dma((2, most - 1)), dma((2, most - 1)),
            dma((2, most - 1)), dma((2, most - 1)),
            dma((2, nx - 1)), dma((2, nx - 1)),
            dma((2, most - 1)), dma((2, most - 1)),
            dma((2 * most,)), dma((2 * most,)),
            dma((2 * most,)), dma((2 * most,)),
            dma((2 * most,)), dma((2 * most,)),
            dma((6,)), dma((6,)),
            dma((nx - 1,)), dma((nx - 1,)),
            dma((3,)),
        ],
        compiler_params=pltpu.CompilerParams(
            collective_id=0, has_side_effects=True, vmem_limit_bytes=VMEM_EXCHANGE
        ),
    )(tab, own, estimate)


def steps_kernel(
    nx, tab, cov_ref, est_ref, out_ref,
    high, low, prec, weights, terms,
):
    blocks, stacked, width = est_ref.shape
    slots = stacked // width
    half = width // 2
    per_x = PAIRS // nx
    f32, bf16 = jnp.float32, jnp.bfloat16

    def row_of(j, s):
        return tab[TABLE + s * blocks + j]

    def count(j):
        return tab[COUNTS + j]

    def holder(q):
        return tab[HOLDER + q]

    def position(i):
        return tab[POSITION + i]

    def pair_of(a, b):
        listed = tab[RANK + jnp.minimum(a, b) * blocks + jnp.maximum(a, b)]
        return listed + jnp.where(a <= b, 0, PAIRS)

    @pl.loop(0, PAIRS)
    def _(t):
        @pl.when((t == 0) | (tab[RIGHT + t] > 0))
        def _():
            u = lax.rem(t, per_x)
            for h in range(2):
                value = cov_ref[t // per_x, h, pl.ds(pl.multiple_of(u * half, 8), half)]
                top = value.astype(bf16)
                high[t, h * half:(h + 1) * half] = top
                low[t, h * half:(h + 1) * half] = (value - top.astype(f32)).astype(bf16)

        @pl.when(tab[LEFT + t] != tab[RIGHT + t])
        def _():
            high[PAIRS + t] = high[t].T
            low[PAIRS + t] = low[t].T

    def block_of(q, s):
        return est_ref[q, pl.ds(pl.multiple_of(s * width, 8), width)]

    def mirror(j, i):
        return jnp.where(row_of(i, 0) == j, 0, jnp.where(row_of(i, 1) == j, 1, 2))

    def products(q, row_blocks, n, dests):
        j = holder(q)
        for i, dest in zip(row_blocks, dests):
            total = None
            for t in range(n):
                pair = pair_of(i, row_of(j, t))
                w = weights[q * slots + t]
                both = jnp.dot(high[pair], w, preferred_element_type=f32) + jnp.dot(
                    low[pair], w, preferred_element_type=f32
                )
                total = both if total is None else total + both
            terms[dest] = total

    def update(q, s, current):
        j = holder(q)
        i = row_of(j, s)
        other = position(i) * slots + mirror(j, i)
        gram = terms[q * slots + s] + terms[other].T
        stepped = current - (0.5 * step_size) * gram
        bound = step_size * penalty
        shrunk = jnp.maximum(stepped - bound, 0.0) + jnp.minimum(stepped + bound, 0.0)
        barrier = 0.5 * (stepped + jnp.sqrt(stepped * stepped + 4.0 * step_size))
        same = lax.broadcasted_iota(jnp.int32, (width, width), 0) == lax.broadcasted_iota(
            jnp.int32, (width, width), 1
        )
        return jnp.where(same & (i == j), barrier, shrunk)

    own_count, own_rows = out_ref.shape[0], out_ref.shape[1]
    own_slot = tab[PLACE + 1]
    first_row = tab[PLACE + 2]
    read = []
    for n in range(own_count):
        q = tab[PLACE] * own_count + n
        read += [q, position(row_of(holder(q), own_slot))]

    def is_read(q):
        return functools.reduce(jnp.logical_or, [q == other for other in read])

    def live_blocks(action, wanted=None):
        @pl.loop(0, blocks * slots)
        def _(flat):
            q, s = flat // slots, lax.rem(flat, slots)
            live = s < count(holder(q))

            @pl.when(live if wanted is None else live & wanted(q))
            def _():
                action(flat, q, s)

    def first_weights(flat, q, s):
        weights[flat] = block_of(q, s).astype(bf16)

    live_blocks(first_weights)

    for iteration in range(ITERS - 1):
        @pl.loop(0, blocks)
        def _(q):
            j = holder(q)
            whole = is_read(q)
            for n in range(1, slots + 1):
                @pl.when(whole & (count(j) == n))
                def _():
                    products(q, [row_of(j, s) for s in range(n)], n, [q * slots + s for s in range(n)])

                for s in range(1, n):
                    i = row_of(j, s)

                    @pl.when(jnp.logical_not(whole) & (count(j) == n) & is_read(position(i)))
                    def _():
                        products(q, [i], n, [q * slots + s])

        def renew(flat, q, s):
            value = update(q, s, block_of(q, s) if iteration == 0 else prec[flat])
            prec[flat] = value
            weights[flat] = value.astype(bf16)

        live_blocks(renew, is_read)

    s = own_slot

    def one_block(q, i, dest):
        for n in range(1, slots + 1):
            @pl.when(count(holder(q)) == n)
            def _():
                products(q, [i], n, [dest])

    for n in range(own_count):
        q = tab[PLACE] * own_count + n
        j = holder(q)
        live = s < count(j)

        @pl.when(live)
        def _():
            i = row_of(j, s)
            qi = position(i)
            one_block(q, i, q * slots + s)

            @pl.when(i != j)
            def _():
                one_block(qi, j, qi * slots + mirror(j, i))

            terms[q * slots + s] = update(q, s, prec[q * slots + s])
            if own_rows % 8 == 0:
                out_ref[n] = terms[q * slots + s, pl.ds(pl.multiple_of(first_row, 8), own_rows)]
            else:
                eight = terms[q * slots + s, pl.ds(pl.multiple_of(first_row // 8 * 8, 8), 8)]
                out_ref[n] = jnp.where(lax.rem(first_row, 8) == 0, eight[:own_rows], eight[8 - own_rows:])

        @pl.when(jnp.logical_not(live))
        def _():
            out_ref[n] = jnp.zeros(out_ref.shape[1:], f32)


def steps(nx, tab, cov, estimate, own_rows):
    blocks, stacked, width = estimate.shape
    count = blocks * (stacked // width)
    f32, bf16 = jnp.float32, jnp.bfloat16
    vmem = pl.BlockSpec(memory_space=pltpu.VMEM)
    smem = pl.BlockSpec(memory_space=pltpu.SMEM)
    return pl.pallas_call(
        functools.partial(steps_kernel, nx),
        out_shape=jax.ShapeDtypeStruct((blocks // nx, own_rows, width), f32),
        in_specs=[smem, vmem, vmem],
        out_specs=vmem,
        scratch_shapes=[
            pltpu.VMEM((2 * PAIRS, width, width), bf16),
            pltpu.VMEM((2 * PAIRS, width, width), bf16),
            pltpu.VMEM((count, width, width), f32),
            pltpu.VMEM((count, width, width), bf16),
            pltpu.VMEM((count, width, width), f32),
        ],
        compiler_params=pltpu.CompilerParams(vmem_limit_bytes=VMEM_STEPS),
    )(tab, cov, estimate)


def pair_tables(block_rows, counts):
    blocks, slots = block_rows.shape
    ids = jnp.arange(blocks, dtype=jnp.int32)
    live = jnp.arange(slots, dtype=jnp.int32)[None, :] < counts[:, None]
    has = jnp.any(live[:, :, None] & (block_rows[:, :, None] == ids), axis=1)
    need = jnp.any(has[:, :, None] & has[:, None, :], axis=0) & (ids[:, None] <= ids[None, :])
    flat = need.reshape(-1).astype(jnp.int32)
    order = jnp.arange(blocks * blocks, dtype=jnp.int32)
    rank = jnp.sum(jnp.where(order[None, :] < order[:, None], flat[None, :], 0), axis=1)
    hit = (flat[None, :] > 0) & (rank[None, :] == jnp.arange(PAIRS, dtype=jnp.int32)[:, None])
    which = jnp.sum(jnp.where(hit, order[None, :], 0), axis=1)
    return which // blocks, which % blocks, rank


def integer_table(block_rows, counts, holder, own_rows, width):
    blocks, slots = block_rows.shape
    columns = sum(
        jnp.pad(part, ((k, slots + 2 - k - part.shape[0]), (0, 0)))
        for k, part in ((0, block_rows.T), (slots, counts[None]), (slots + 1, holder[None]))
    )
    columns = lax.optimization_barrier(columns)
    raw = columns.reshape(-1)
    left, right, rank = pair_tables(columns[:slots].T, columns[slots])
    ids = jnp.arange(blocks, dtype=jnp.int32)
    position = jnp.sum(jnp.where(columns[slots + 1][:, None] == ids[None, :], ids[:, None], 0), axis=0)
    first = lax.axis_index("samp") * own_rows
    place = jnp.stack([lax.axis_index("var"), first // width, first % width]).astype(jnp.int32)
    return jnp.concatenate([raw, position, rank, left, right, place])


def body(dims, samples, estimate, block_rows, counts, holder):
    nx, ny, nz = dims
    rows_dev, _, width = samples.shape
    samp_count = 2 * ny * nz
    own_rows = block_rows.shape[1] * width // samp_count
    tab = integer_table(block_rows, counts, holder, own_rows, width)
    own = samples.transpose(1, 0, 2)
    cov, every = exchange(dims, rows_dev * samp_count, tab, own, pltpu.with_memory_space_constraint(estimate, pltpu.HBM))
    return steps(nx, tab, cov, every, own_rows)


def solution(mesh):
    nx = mesh.shape["var"]
    ny, nz = (8, 12) if mesh.shape["samp"] == 192 else (2, 2)
    return jax.shard_map(
        functools.partial(body, (nx, ny, nz)),
        mesh=mesh,
        in_specs=(P("samp", "var", None), P("var", None, None), P(), P(), P()),
        out_specs=P("var", "samp", None),
        check_vma=False,
    )
```
